256 devices in a mesh: cell: 32 (over z_lo, y, core), gene: 8 (over z_hi, x).
Axes of the slice: x: 4, y: 4, z: 8 (z_hi: 2, z_lo: 4; z = z_hi * 4 + z_lo), core: 2. Of those that a mesh axis runs over, the one named last changes fastest.
Arguments:
- counts: bfloat16 [65536, 16384], P('cell', 'gene'), may hold values from 0 to 25, as said below
- cell_factor: float32 [32, 65536], P(None, 'cell'), may hold values from 0.15 to 4.5, as said below
- gene_factor: float32 [32, 16384], P(None, 'gene'), may hold values from 0.15 to 4.5, as said below
Outputs:
- cell_result: float32 [32, 65536], P(None, 'cell')
- gene_result: float32 [32, 16384], P(None, 'gene')
The draws below stay inside these ranges and needn't reach their ends.
Inputs may be any that keep to these rules, and one draw needn't show every extreme that they name: `counts`: whole numbers. `cell_factor`: positive. `gene_factor`: positive.
All inputs are finite; a program needn't handle non-finite values.
Results may differ from the reference program's by a relative error of at most 0.001.
Values sent between devices are 32-bit elements; how exact they have to be, the bound alone decides.
No kernel may reach another device: no remote copies, remote signals or barrier semaphores. Data moves between devices by JAX's collectives and lax.ppermute only.
A program may use at most 64 MiB of HBM per device.

```python
import math
import jax
import jax.numpy as jnp
from jax import lax

RANK = 32
GENES = 16384
ROWS_DEV = 2048
ITERS = 3
CELLS = 65536
N_CELL = 32


def positive_factor(key, length):
    rise = 1.0 + 2.0 * jnp.arange(length, dtype=jnp.float32) / max(length - 1, 1)
    base = 0.5 * jnp.exp(jax.random.uniform(key, (RANK, length), jnp.float32, math.log(0.3), math.log(3.0)))
    return base * rise[None, :]


def draw_counts(key, part):
    key = jax.random.fold_in(key, 11)
    first, second, third = jax.random.split(key, 3)
    row_level = jax.random.randint(first, (CELLS, 1), 1, 9)
    col_level = jax.random.randint(second, (1, GENES), 1, 4)
    values = jax.random.randint(third, (CELLS, GENES), 0, 1 + row_level * col_level)
    return values.astype(jnp.float32).astype(jnp.bfloat16)


def draw_cell_factor(key, part):
    key = jax.random.fold_in(key, 23)
    return positive_factor(key, CELLS)


def draw_gene_factor(key, part):
    key = jax.random.fold_in(key, 37)
    return positive_factor(key, GENES)


def setup_inputs(seed: int = 0) -> dict:
    keys = jax.random.split(jax.random.key(seed), 4)
    return {
        "counts": draw_counts(jax.random.fold_in(keys[3], 71), 0),
        "cell_factor": draw_cell_factor(jax.random.fold_in(keys[3], 71), 0),
        "gene_factor": draw_gene_factor(jax.random.fold_in(keys[3], 71), 0),
    }


def ratio_block(block, cell_copy, gene_copy):
    approx = lax.dot_general(cell_copy, gene_copy, (((0,), (0,)), ((), ())), preferred_element_type=jnp.float32)
    return (block.astype(jnp.float32) / approx).astype(jnp.bfloat16)


def reference(counts, cell_factor, gene_factor):
    blocks = counts.reshape(N_CELL, ROWS_DEV, GENES)
    factor_now = cell_factor
    gene_now = gene_factor
    for step in range(ITERS):
        pieces = jnp.transpose(factor_now.reshape(RANK, N_CELL, ROWS_DEV), (1, 0, 2))
        gene_copy = gene_now.astype(jnp.bfloat16)

        def gene_pass(total, pair):
            block, piece = pair
            cell_copy = piece.astype(jnp.bfloat16)
            ratio = ratio_block(block, cell_copy, gene_copy)
            return total + jnp.dot(cell_copy, ratio, preferred_element_type=jnp.float32), None

        numerator = lax.scan(gene_pass, jnp.zeros((RANK, GENES), jnp.float32), (blocks, pieces))[0]
        denominator = jnp.sum(factor_now, axis=1)
        gene_now = gene_now * numerator / denominator[:, None]
        new_copy = gene_now.astype(jnp.bfloat16)

        def cell_pass(pair):
            block, piece = pair
            ratio = ratio_block(block, piece.astype(jnp.bfloat16), new_copy)
            return lax.dot_general(new_copy, ratio, (((1,), (1,)), ((), ())), preferred_element_type=jnp.float32)

        parts = lax.map(cell_pass, (blocks, pieces))
        cell_numer = jnp.transpose(parts, (1, 0, 2)).reshape(RANK, CELLS)
        cell_denom = jnp.sum(gene_now, axis=1)
        factor_now = factor_now * cell_numer / cell_denom[:, None]
    return factor_now, gene_now
```

```python
import functools

import jax
import jax.numpy as jnp
from jax import lax
from jax.experimental import pallas as pl
from jax.experimental.pallas import tpu as pltpu
from jax.sharding import PartitionSpec as P

ITERS = 3
RANK = 32
GROUPS = 4
LANES = 128
TILE = 256
CORES, Y, X = 2, 4, 4
F32, BF16 = jnp.float32, jnp.bfloat16

AT_CORE, AT_Y, AT_Z, AT_X = range(4)


def struct(shape, dtype=F32):
    return jax.ShapeDtypeStruct(shape, dtype)


def small_call(kernel, info, operands, out_shape, scratch=()):
    return pl.pallas_call(
        kernel,
        grid_spec=pltpu.PrefetchScalarGridSpec(
            num_scalar_prefetch=1,
            grid=(),
            in_specs=[pl.BlockSpec(memory_space=pltpu.VMEM)] * len(operands),
            out_specs=jax.tree.map(lambda _: pl.BlockSpec(memory_space=pltpu.VMEM), out_shape),
            scratch_shapes=list(scratch),
        ),
        out_shape=out_shape,
        compiler_params=pltpu.CompilerParams(vmem_limit_bytes=4 << 20),
    )(info, *operands)


def pass_params():
    return pltpu.CompilerParams(vmem_limit_bytes=20 << 20)


def pass_cost(cells, genes):
    return pl.CostEstimate(flops=4 * cells * genes * RANK * 4, bytes_accessed=2 * cells * genes, transcendentals=0)


def ratio_of(counts, approx):
    return (counts.astype(F32) * pl.reciprocal(approx, approx=True)).astype(BF16)


def block_index(mine, step):
    return lax.rem(mine + step, 4)


def gene_block(counts_ref, cell_copy, cell_turned, sums, gene_refs, out_ref, turn):
    j = pl.program_id(0)
    rows_of_groups = jnp.stack([ref[...] for ref in gene_refs])
    genes = turn(rows_of_groups).reshape(RANK, TILE).astype(BF16)
    numer = jnp.zeros((RANK, TILE), F32)
    for start in range(0, counts_ref.shape[0], TILE):
        rows = slice(start, start + TILE)
        approx = jnp.dot(cell_turned[rows, :], genes, preferred_element_type=F32)
        ratio = ratio_of(counts_ref[rows, :], approx)
        numer = numer + jnp.dot(cell_copy[:, rows], ratio, preferred_element_type=F32)
    at = pl.multiple_of(j * TILE, TILE)
    out_ref[:, :, pl.ds(at, TILE)] = numer.reshape(GROUPS, 8, TILE)

    @pl.when(j == 0)
    def _():
        out_ref[:, :, out_ref.shape[2] - LANES :] = sums[...].reshape(GROUPS, 8, LANES)


def in_order(info, scratch):
    def turn(groups):
        for s in range(GROUPS):
            scratch[block_index(info[AT_Y], GROUPS - s)] = groups[s]
        return scratch[...]

    return turn


def gene_first_kernel(info, counts_ref, f0, f1, f2, f3, g0, g1, g2, g3, out_ref, cell_copy, cell_turned, sums, ordered):
    quarter = f0.shape[1]

    @pl.when(pl.program_id(0) == 0)
    def _():
        total = jnp.zeros((RANK, 1), F32)
        for s, ref in enumerate((f0, f1, f2, f3)):
            piece = ref[...]
            at = pl.multiple_of(block_index(info[AT_X], X - s) * quarter, quarter)
            cell_copy[:, pl.ds(at, quarter)] = piece.astype(BF16)
            cell_turned[pl.ds(at, quarter), :] = piece.T.astype(BF16)
            total = total + jnp.sum(piece, axis=1, keepdims=True)
        sums[...] = jnp.broadcast_to(total, (RANK, LANES))

    gene_block(counts_ref, cell_copy, cell_turned, sums, (g0, g1, g2, g3), out_ref, in_order(info, ordered))


def gene_second_kernel(info, counts_ref, cell_copy, cell_turned, sums, g0, g1, g2, g3, out_ref, ordered):
    gene_block(counts_ref, cell_copy, cell_turned, sums, (g0, g1, g2, g3), out_ref, in_order(info, ordered))


def gene_half(info, counts, mine, left, genes):
    first = len(left) == 4
    n_cells, n_genes = counts.shape
    half = n_genes // CORES
    blocks = half // TILE
    which = (lambda info: info[AT_CORE]) if mine else (lambda info: 1 - info[AT_CORE])

    def whole(shape):
        return pl.BlockSpec(shape, lambda j, info: (0,) * len(shape))

    made = (struct((RANK, n_cells), BF16), struct((n_cells, RANK), BF16), struct((RANK, LANES)))
    sums = struct((GROUPS, 8, half + LANES))
    outs = (sums,) + made if first else (sums,)
    return pl.pallas_call(
        gene_first_kernel if first else gene_second_kernel,
        grid_spec=pltpu.PrefetchScalarGridSpec(
            num_scalar_prefetch=1,
            grid=(blocks,),
            in_specs=[pl.BlockSpec((n_cells, TILE), lambda j, info: (0, which(info) * blocks + j))]
            + [whole(a.shape) for a in left]
            + [pl.BlockSpec((8, TILE), lambda j, info: (0, j))] * GROUPS,
            out_specs=[whole(o.shape) for o in outs],
            scratch_shapes=[pltpu.VMEM((GROUPS, 8, TILE), F32)],
        ),
        out_shape=outs,
        compiler_params=pass_params(),
        cost_estimate=pass_cost(n_cells, half),
    )(info, counts, *left, *genes)


def cell_block(counts_ref, cell_ref, gene_copy, sums, out_ref):
    i = pl.program_id(0)
    cells = cell_ref[...].T.astype(BF16)
    numer = jnp.zeros((TILE, RANK), F32)
    for start in range(0, counts_ref.shape[1], TILE):
        cols = slice(start, start + TILE)
        genes = gene_copy[:, cols]
        approx = jnp.dot(cells, genes, preferred_element_type=F32)
        ratio = ratio_of(counts_ref[:, cols], approx)
        numer = numer + lax.dot_general(ratio, genes, (((1,), (1,)), ((), ())), preferred_element_type=F32)
    at = pl.multiple_of(i * TILE, TILE)
    out_ref[:, pl.ds(at, TILE)] = numer.T

    @pl.when(i == 0)
    def _():
        out_ref[:, out_ref.shape[1] - LANES :] = sums[...]


def cell_first_kernel(info, counts_ref, cell_ref, *refs):
    gene_refs, (out_ref, gene_copy, sums, ordered) = refs[: 2 * GROUPS], refs[2 * GROUPS :]
    half = gene_refs[0].shape[1]

    @pl.when(pl.program_id(0) == 0)
    def _():
        for s, ref in enumerate(gene_refs):
            side = info[AT_CORE] if s < GROUPS else 1 - info[AT_CORE]
            at = pl.multiple_of(side * half, half)
            ordered[block_index(info[AT_Y], GROUPS - s % GROUPS), :, pl.ds(at, half)] = ref[...]
        genes = ordered[...].reshape(RANK, CORES * half)
        gene_copy[...] = genes.astype(BF16)
        sums[...] = jnp.broadcast_to(jnp.sum(genes, axis=1, keepdims=True), (RANK, LANES))

    cell_block(counts_ref, cell_ref, gene_copy, sums, out_ref)


def cell_later_kernel(info, counts_ref, cell_ref, gene_copy, sums, out_ref):
    cell_block(counts_ref, cell_ref, gene_copy, sums, out_ref)


def cell_quarter(info, counts, to, cells, left):
    first = len(left) == 2 * GROUPS
    n_cells, n_genes = counts.shape
    quarter = n_cells // X
    blocks = quarter // TILE

    def whole(shape):
        return pl.BlockSpec(shape, lambda i, info: (0,) * len(shape))

    made = (struct((RANK, n_genes), BF16), struct((RANK, LANES)))
    sums = struct((RANK, quarter + LANES))
    outs = (sums,) + made if first else (sums,)
    return pl.pallas_call(
        cell_first_kernel if first else cell_later_kernel,
        grid_spec=pltpu.PrefetchScalarGridSpec(
            num_scalar_prefetch=1,
            grid=(blocks,),
            in_specs=[
                pl.BlockSpec((TILE, n_genes), lambda i, info: (block_index(info[AT_X], to) * blocks + i, 0)),
                pl.BlockSpec((RANK, TILE), lambda i, info: (0, i)),
            ]
            + [whole(a.shape) for a in left],
            out_specs=[whole(o.shape) for o in outs],
            scratch_shapes=[pltpu.VMEM((GROUPS, 8, n_genes), F32)] if first else [],
        ),
        out_shape=outs,
        compiler_params=pass_params(),
        cost_estimate=pass_cost(quarter, n_genes),
    )(info, counts, cells, *left)


def pair_sum_kernel(info, a_ref, b_ref, *out_refs):
    for s, out_ref in enumerate(out_refs):
        g = block_index(info[AT_Y], s)
        out_ref[...] = a_ref[g] + b_ref[g]


def four_sum_kernel(info, a_ref, b_ref, c_ref, d_ref, out_ref):
    out_ref[...] = (a_ref[...] + b_ref[...]) + (c_ref[...] + d_ref[...])


def updated(piece, total):
    width = piece.shape[1]
    return piece * total[:, :width] / total[:, width : width + 1]


def gene_update_kernel(n_z, info, piece_ref, *refs):
    terms, (out_ref, ordered) = refs[:n_z], refs[n_z:]
    for s, ref in enumerate(terms):
        ordered[lax.rem(info[AT_Z] + (n_z - s), n_z)] = ref[...]
    total = ordered[0]
    for s in range(1, n_z):
        total = total + ordered[s]
    out_ref[...] = updated(piece_ref[...], total)


def cell_update_kernel(info, piece_ref, *refs):
    total = refs[0][...]
    for ref in refs[1:-1]:
        total = total + ref[...]
    refs[-1][...] = updated(piece_ref[...], total)


def cut_kernel(info, cell_ref, gene_ref, *out_refs):
    quarter, half = cell_ref.shape[1] // X, gene_ref.shape[2] // CORES
    for s in range(X):
        at = pl.multiple_of(block_index(info[AT_X], X - s) * quarter, quarter)
        out_refs[s][...] = cell_ref[:, pl.ds(at, quarter)]
    for s in range(2 * GROUPS):
        side = info[AT_CORE] if s < GROUPS else 1 - info[AT_CORE]
        at = pl.multiple_of(side * half, half)
        out_refs[X + s][...] = gene_ref[block_index(info[AT_Y], GROUPS - s % GROUPS), :, pl.ds(at, half)]


def join_cells_kernel(info, *refs):
    out_ref = refs[-1]
    quarter = refs[0].shape[1]
    for s, ref in enumerate(refs[:-1]):
        at = pl.multiple_of(block_index(info[AT_X], X - s) * quarter, quarter)
        out_ref[:, pl.ds(at, quarter)] = ref[...]


def join_genes_kernel(info, *refs):
    out_ref = refs[-1]
    half = refs[0].shape[1]
    for s, ref in enumerate(refs[:-1]):
        side = info[AT_CORE] if s < GROUPS else 1 - info[AT_CORE]
        at = pl.multiple_of(side * half, half)
        out_ref[block_index(info[AT_Y], GROUPS - s % GROUPS), :, pl.ds(at, half)] = ref[...]


def per_device(n_cell, n_gene, counts, cell_factor, gene_factor):
    n_z, n_zhi = n_cell // (Y * CORES), n_gene // X
    n_cells, n_genes = counts.shape
    quarter, half = n_cells // X, n_genes // CORES
    cell_at, gene_at = lax.axis_index("cell"), lax.axis_index("gene")
    info = jnp.stack([cell_at % CORES, cell_at // CORES % Y, cell_at // (CORES * Y), gene_at % X]).astype(jnp.int32)

    def to_core(a):
        return lax.ppermute(a, "cell", [(i, i ^ 1) for i in range(n_cell)])

    def to_y(a, s):
        step = lambda i: i - i % (Y * CORES) + (i + s * CORES) % (Y * CORES)
        return lax.ppermute(a, "cell", [(i, step(i)) for i in range(n_cell)])

    def to_z(a, s):
        return lax.ppermute(a, "cell", [(i, (i + s * Y * CORES) % n_cell) for i in range(n_cell)])

    def to_x(a, s):
        return lax.ppermute(a, "gene", [(i, i - i % X + (i + s) % X) for i in range(n_gene)])

    def to_zhi(a, s):
        return lax.ppermute(a, "gene", [(i, (i + s * X) % n_gene) for i in range(n_gene)])

    pieces = small_call(
        cut_kernel,
        info,
        (cell_factor, gene_factor.reshape(GROUPS, 8, n_genes)),
        [struct((RANK, quarter))] * X + [struct((8, half))] * (2 * GROUPS),
    )
    cells, mine, other = pieces[:X], pieces[X : X + GROUPS], pieces[X + GROUPS :]
    piece, wide = struct((8, half)), half + LANES
    for step in range(ITERS):
        sent, *left = gene_half(info, counts, False, cells, other)
        got = to_core(sent)
        kept = gene_half(info, counts, True, left, mine)[0]
        parts = small_call(pair_sum_kernel, info, (kept, got), [struct((8, wide))] * Y)
        got = [to_y(parts[s], s) for s in (1, 2, 3)]
        part = small_call(four_sum_kernel, info, (parts[0], *got), struct((8, wide)))
        got = [to_z(part, s) for s in range(1, n_z)]
        new = small_call(
            functools.partial(gene_update_kernel, n_z),
            info,
            (mine[0], part, *got),
            piece,
            [pltpu.VMEM((n_z, 8, wide), F32)],
        )
        mine = [new] + [to_y(new, s) for s in (1, 2, 3)]
        other = [to_core(a) for a in mine]

        left = (*mine, *other)
        got = {}
        for s in (2, 1, 3, 0):
            sums, *made = cell_quarter(info, counts, s, cells[(X - s) % X], left)
            left = made or left
            got[s] = to_x(sums, s) if s else sums
        part = small_call(four_sum_kernel, info, [got[s] for s in range(X)], struct((RANK, quarter + LANES)))
        got = [to_zhi(part, s) for s in range(1, n_zhi)]
        new = small_call(cell_update_kernel, info, (cells[0], part, *got), struct((RANK, quarter)))
        cells = [new] + [to_x(new, s) for s in (1, 2, 3)]
    genes = small_call(join_genes_kernel, info, (*mine, *other), struct((GROUPS, 8, n_genes)))
    cells = small_call(join_cells_kernel, info, cells, struct((RANK, n_cells)))
    return cells, genes.reshape(RANK, n_genes)


def solution(mesh):
    return jax.shard_map(
        functools.partial(per_device, mesh.shape["cell"], mesh.shape["gene"]),
        mesh=mesh,
        in_specs=(P("cell", "gene"), P(None, "cell"), P(None, "gene")),
        out_specs=(P(None, "cell"), P(None, "gene")),
        check_vma=False,
    )
```

```python
import functools

import jax
import jax.numpy as jnp
from jax import lax
from jax.experimental import pallas as pl
from jax.experimental.pallas import tpu as pltpu
from jax.sharding import PartitionSpec as P

ITERS = 3
RANK = 32
GROUPS = 4
LANES = 128
TILE, WIDE = 256, 512
SMALL_VMEM, PASS_VMEM = 4 << 20, 24 << 20
CORES, Y, X = 2, 4, 4
F32, BF16 = jnp.float32, jnp.bfloat16

AT_CORE, AT_Y, AT_Z, AT_X = range(4)


def struct(shape, dtype=F32):
    return jax.ShapeDtypeStruct(shape, dtype)


def kernel_call(kernel, info, operands, out_shape, scratch=(), vmem=SMALL_VMEM, cost=None):
    return pl.pallas_call(
        kernel,
        grid_spec=pltpu.PrefetchScalarGridSpec(
            num_scalar_prefetch=1,
            grid=(),
            in_specs=[pl.BlockSpec(memory_space=pltpu.VMEM)] * len(operands),
            out_specs=jax.tree.map(lambda _: pl.BlockSpec(memory_space=pltpu.VMEM), out_shape),
            scratch_shapes=list(scratch),
        ),
        out_shape=out_shape,
        compiler_params=pltpu.CompilerParams(vmem_limit_bytes=vmem),
        cost_estimate=cost,
    )(info, *operands)


def pass_cost(cells, genes):
    return pl.CostEstimate(flops=cells * genes, bytes_accessed=cells * genes // 8, transcendentals=0)


def ratio_of(counts, approx):
    return (counts.astype(F32) * pl.reciprocal(approx, approx=True)).astype(BF16)


def block_index(mine, step):
    return lax.rem(mine + step, 4)


def gene_block(side, counts_ref, cell_copy, cell_turned, sums, groups, out_ref):
    n_cells = counts_ref.shape[0]
    half = out_ref.shape[2] - LANES
    base = side * half

    @pl.loop(0, half // WIDE)
    def _(j):
        at = pl.multiple_of(j * WIDE, WIDE)
        cols = pl.ds(pl.multiple_of(base + at, WIDE), WIDE)
        genes = groups[:, :, pl.ds(at, WIDE)].reshape(RANK, WIDE).astype(BF16)
        numer = jnp.zeros((RANK, WIDE), F32)
        for start in range(0, n_cells, TILE):
            rows = slice(start, start + TILE)
            approx = jnp.dot(cell_turned[rows, :], genes, preferred_element_type=F32)
            ratio = ratio_of(counts_ref[rows, cols], approx)
            numer = numer + jnp.dot(cell_copy[:, rows], ratio, preferred_element_type=F32)
        out_ref[:, :, pl.ds(at, WIDE)] = numer.reshape(GROUPS, 8, WIDE)

    out_ref[:, :, half:] = sums[...].reshape(GROUPS, 8, LANES)


def set_groups(info, gene_refs, groups):
    for s, ref in enumerate(gene_refs):
        groups[block_index(info[AT_Y], GROUPS - s)] = ref[...]


def gene_first_kernel(info, counts_ref, f0, f1, f2, f3, g0, g1, g2, g3, out_ref, cell_copy, cell_turned, sums, groups):
    quarter = f0.shape[1]
    total = jnp.zeros((RANK, 1), F32)
    for s, ref in enumerate((f0, f1, f2, f3)):
        piece = ref[...]
        at = pl.multiple_of(block_index(info[AT_X], X - s) * quarter, quarter)
        cell_copy[:, pl.ds(at, quarter)] = piece.astype(BF16)
        cell_turned[pl.ds(at, quarter), :] = piece.T.astype(BF16)
        total = total + jnp.sum(piece, axis=1, keepdims=True)
    sums[...] = jnp.broadcast_to(total, (RANK, LANES))
    set_groups(info, (g0, g1, g2, g3), groups)
    gene_block(1 - info[AT_CORE], counts_ref, cell_copy, cell_turned, sums, groups, out_ref)


def gene_second_kernel(info, counts_ref, cell_copy, cell_turned, sums, g0, g1, g2, g3, out_ref, groups):
    set_groups(info, (g0, g1, g2, g3), groups)
    gene_block(info[AT_CORE], counts_ref, cell_copy, cell_turned, sums, groups, out_ref)


def gene_half(info, counts, left, genes):
    first = len(left) == 4
    n_cells, n_genes = counts.shape
    half = n_genes // CORES
    sums = struct((GROUPS, 8, half + LANES))
    made = [struct((RANK, n_cells), BF16), struct((n_cells, RANK), BF16), struct((RANK, LANES))]
    return kernel_call(
        gene_first_kernel if first else gene_second_kernel,
        info,
        (counts, *left, *genes),
        [sums] + made if first else [sums],
        [pltpu.VMEM((GROUPS, 8, half), F32)],
        PASS_VMEM,
        pass_cost(n_cells, half),
    )


def cell_block(to, info, counts_ref, cell_ref, gene_copy, sums, out_ref):
    quarter = cell_ref.shape[1]
    base = block_index(info[AT_X], to) * quarter

    @pl.loop(0, quarter // TILE)
    def _(i):
        at = pl.multiple_of(i * TILE, TILE)
        rows = pl.ds(pl.multiple_of(base + at, TILE), TILE)
        cells = cell_ref[:, pl.ds(at, TILE)].T.astype(BF16)
        numer = jnp.zeros((TILE, RANK), F32)
        for start in range(0, counts_ref.shape[1], WIDE):
            cols = slice(start, start + WIDE)
            genes = gene_copy[:, cols]
            approx = jnp.dot(cells, genes, preferred_element_type=F32)
            ratio = ratio_of(counts_ref[rows, cols], approx)
            numer = numer + lax.dot_general(ratio, genes, (((1,), (1,)), ((), ())), preferred_element_type=F32)
        out_ref[:, pl.ds(at, TILE)] = numer.T

    out_ref[:, quarter:] = sums[...]


def cell_first_kernel(to, info, counts_ref, cell_ref, *refs):
    gene_refs, (out_ref, gene_copy, sums, ordered) = refs[: 2 * GROUPS], refs[2 * GROUPS :]
    half = gene_refs[0].shape[1]
    for s, ref in enumerate(gene_refs):
        side = info[AT_CORE] if s < GROUPS else 1 - info[AT_CORE]
        at = pl.multiple_of(side * half, half)
        ordered[block_index(info[AT_Y], GROUPS - s % GROUPS), :, pl.ds(at, half)] = ref[...]
    genes = ordered[...].reshape(RANK, CORES * half)
    gene_copy[...] = genes.astype(BF16)
    sums[...] = jnp.broadcast_to(jnp.sum(genes, axis=1, keepdims=True), (RANK, LANES))
    cell_block(to, info, counts_ref, cell_ref, gene_copy, sums, out_ref)


def cell_quarter(info, counts, to, cells, left):
    first = len(left) == 2 * GROUPS
    n_cells, n_genes = counts.shape
    quarter = n_cells // X
    sums = struct((RANK, quarter + LANES))
    made = [struct((RANK, n_genes), BF16), struct((RANK, LANES))]
    return kernel_call(
        functools.partial(cell_first_kernel if first else cell_block, to),
        info,
        (counts, cells, *left),
        [sums] + made if first else [sums],
        [pltpu.VMEM((GROUPS, 8, n_genes), F32)] if first else [],
        PASS_VMEM,
        pass_cost(quarter, n_genes),
    )


def pair_sum_kernel(info, a_ref, b_ref, *out_refs):
    for s, out_ref in enumerate(out_refs):
        g = block_index(info[AT_Y], s)
        out_ref[...] = a_ref[g] + b_ref[g]


def four_sum_kernel(info, a_ref, b_ref, c_ref, d_ref, out_ref):
    out_ref[...] = (a_ref[...] + b_ref[...]) + (c_ref[...] + d_ref[...])


def updated(piece, total):
    width = piece.shape[1]
    return piece * total[:, :width] / total[:, width : width + 1]


def gene_update_kernel(n_z, info, piece_ref, *refs):
    terms, (out_ref, ordered) = refs[:n_z], refs[n_z:]
    for s, ref in enumerate(terms):
        ordered[lax.rem(info[AT_Z] + (n_z - s), n_z)] = ref[...]
    total = ordered[0]
    for s in range(1, n_z):
        total = total + ordered[s]
    out_ref[...] = updated(piece_ref[...], total)


def cell_update_kernel(info, piece_ref, *refs):
    total = refs[0][...]
    for ref in refs[1:-1]:
        total = total + ref[...]
    refs[-1][...] = updated(piece_ref[...], total)


def cut_kernel(info, cell_ref, gene_ref, *out_refs):
    quarter, half = cell_ref.shape[1] // X, gene_ref.shape[2] // CORES
    for s in range(X):
        at = pl.multiple_of(block_index(info[AT_X], X - s) * quarter, quarter)
        out_refs[s][...] = cell_ref[:, pl.ds(at, quarter)]
    for s in range(2 * GROUPS):
        side = info[AT_CORE] if s < GROUPS else 1 - info[AT_CORE]
        at = pl.multiple_of(side * half, half)
        out_refs[X + s][...] = gene_ref[block_index(info[AT_Y], GROUPS - s % GROUPS), :, pl.ds(at, half)]


def join_cells_kernel(info, *refs):
    out_ref = refs[-1]
    quarter = refs[0].shape[1]
    for s, ref in enumerate(refs[:-1]):
        at = pl.multiple_of(block_index(info[AT_X], X - s) * quarter, quarter)
        out_ref[:, pl.ds(at, quarter)] = ref[...]


def join_genes_kernel(info, *refs):
    out_ref = refs[-1]
    half = refs[0].shape[1]
    for s, ref in enumerate(refs[:-1]):
        side = info[AT_CORE] if s < GROUPS else 1 - info[AT_CORE]
        at = pl.multiple_of(side * half, half)
        out_ref[block_index(info[AT_Y], GROUPS - s % GROUPS), :, pl.ds(at, half)] = ref[...]


def per_device(n_cell, n_gene, counts, cell_factor, gene_factor):
    n_z, n_zhi = n_cell // (Y * CORES), n_gene // X
    n_cells, n_genes = counts.shape
    quarter, half = n_cells // X, n_genes // CORES
    cell_at, gene_at = lax.axis_index("cell"), lax.axis_index("gene")
    info = jnp.stack([cell_at % CORES, cell_at // CORES % Y, cell_at // (CORES * Y), gene_at % X]).astype(jnp.int32)

    def to_core(a):
        return lax.ppermute(a, "cell", [(i, i ^ 1) for i in range(n_cell)])

    def to_y(a, s):
        step = lambda i: i - i % (Y * CORES) + (i + s * CORES) % (Y * CORES)
        return lax.ppermute(a, "cell", [(i, step(i)) for i in range(n_cell)])

    def to_z(a, s):
        return lax.ppermute(a, "cell", [(i, (i + s * Y * CORES) % n_cell) for i in range(n_cell)])

    def to_x(a, s):
        return lax.ppermute(a, "gene", [(i, i - i % X + (i + s) % X) for i in range(n_gene)])

    def to_zhi(a, s):
        return lax.ppermute(a, "gene", [(i, (i + s * X) % n_gene) for i in range(n_gene)])

    pieces = kernel_call(
        cut_kernel,
        info,
        (cell_factor, gene_factor.reshape(GROUPS, 8, n_genes)),
        [struct((RANK, quarter))] * X + [struct((8, half))] * (2 * GROUPS),
    )
    cells, mine, other = pieces[:X], pieces[X : X + GROUPS], pieces[X + GROUPS :]
    piece, wide = struct((8, half)), half + LANES
    for step in range(ITERS):
        sent, *left = gene_half(info, counts, cells, other)
        got = to_core(sent)
        kept = gene_half(info, counts, left, mine)[0]
        parts = kernel_call(pair_sum_kernel, info, (kept, got), [struct((8, wide))] * Y)
        got = [to_y(parts[s], s) for s in (1, 2, 3)]
        part = kernel_call(four_sum_kernel, info, (parts[0], *got), struct((8, wide)))
        got = [to_z(part, s) for s in range(1, n_z)]
        new = kernel_call(
            functools.partial(gene_update_kernel, n_z),
            info,
            (mine[0], part, *got),
            piece,
            [pltpu.VMEM((n_z, 8, wide), F32)],
        )
        mine = [new] + [to_y(new, s) for s in (1, 2, 3)]
        other = [to_core(a) for a in mine]

        left = (*mine, *other)
        got = {}
        for s in (2, 1, 3, 0):
            sums, *made = cell_quarter(info, counts, s, cells[(X - s) % X], left)
            sums, left = lax.optimization_barrier((sums, made or left))
            got[s] = to_x(sums, s) if s else sums
        part = kernel_call(four_sum_kernel, info, [got[s] for s in range(X)], struct((RANK, quarter + LANES)))
        got = [to_zhi(part, s) for s in range(1, n_zhi)]
        new = kernel_call(cell_update_kernel, info, (cells[0], part, *got), struct((RANK, quarter)))
        cells = [new] + [to_x(new, s) for s in (1, 2, 3)]
    genes = kernel_call(join_genes_kernel, info, (*mine, *other), struct((GROUPS, 8, n_genes)))
    cells = kernel_call(join_cells_kernel, info, cells, struct((RANK, n_cells)))
    return cells, genes.reshape(RANK, n_genes)


def solution(mesh):
    return jax.shard_map(
        functools.partial(per_device, mesh.shape["cell"], mesh.shape["gene"]),
        mesh=mesh,
        in_specs=(P("cell", "gene"), P(None, "cell"), P(None, "gene")),
        out_specs=(P(None, "cell"), P(None, "gene")),
        check_vma=False,
    )
```

```python
import functools

import jax
import jax.numpy as jnp
from jax import lax
from jax.experimental import pallas as pl
from jax.experimental.pallas import tpu as pltpu
from jax.sharding import Mesh
from jax.sharding import PartitionSpec as P

ITERS = 3
RANK = 32
GROUPS = 4
LANES = 128
TILE, WIDE, HIGH = 256, 1024, 512
CORES, Y, X = 2, 4, 4
SMALL_VMEM, PASS_VMEM = 4 << 20, 28 << 20
F32, BF16 = jnp.float32, jnp.bfloat16

AT_CORE, AT_Y, AT_X = range(3)


def struct(shape, dtype=F32):
    return jax.ShapeDtypeStruct(shape, dtype)


def kernel_call(kernel, info, operands, out_shape, scratch=(), vmem=SMALL_VMEM, cost=None):
    return pl.pallas_call(
        kernel,
        grid_spec=pltpu.PrefetchScalarGridSpec(
            num_scalar_prefetch=1,
            grid=(),
            in_specs=[pl.BlockSpec(memory_space=pltpu.VMEM)] * len(operands),
            out_specs=jax.tree.map(lambda _: pl.BlockSpec(memory_space=pltpu.VMEM), out_shape),
            scratch_shapes=list(scratch),
        ),
        out_shape=out_shape,
        compiler_params=pltpu.CompilerParams(vmem_limit_bytes=vmem),
        cost_estimate=cost,
    )(info, *operands)


def pass_cost(cells, genes):
    return pl.CostEstimate(flops=cells * genes, bytes_accessed=cells * genes // 8, transcendentals=0)


def ratio_of(counts, approx):
    return (counts.astype(F32) * pl.reciprocal(approx, approx=True)).astype(BF16)


def half_of(info, refs, mine):
    if len(refs) == 2:
        return refs[0 if mine else 1]
    half = refs[0].shape[2] // CORES
    side = info[AT_CORE] if mine else 1 - info[AT_CORE]
    return refs[0].at[:, :, pl.ds(pl.multiple_of(side * half, half), half)]


def gene_block(side, counts_ref, cell_copy, cell_turned, sums, groups, out_ref):
    n_cells = counts_ref.shape[0]
    half = out_ref.shape[2] - LANES
    base = side * half

    @pl.loop(0, half // WIDE)
    def _(j):
        at = pl.multiple_of(j * WIDE, WIDE)
        cols = pl.ds(pl.multiple_of(base + at, WIDE), WIDE)
        genes = groups[:, :, pl.ds(at, WIDE)].reshape(RANK, WIDE).astype(BF16)
        numer = jnp.zeros((RANK, WIDE), F32)
        for start in range(0, n_cells, TILE):
            rows = slice(start, start + TILE)
            approx = jnp.dot(cell_turned[rows, :], genes, preferred_element_type=F32)
            ratio = ratio_of(counts_ref[rows, cols], approx)
            numer = numer + jnp.dot(cell_copy[:, rows], ratio, preferred_element_type=F32)
        out_ref[:, :, pl.ds(at, WIDE)] = numer.reshape(GROUPS, 8, WIDE)

    out_ref[:, :, half:] = sums[...].reshape(GROUPS, 8, LANES)


def gene_first_kernel(info, counts_ref, cells_ref, *refs):
    gene_refs, (out_ref, cell_copy, cell_turned, sums) = refs[:-4], refs[-4:]
    cells = cells_ref[...].reshape(RANK, cells_ref.shape[2])
    cell_copy[...] = cells.astype(BF16)
    cell_turned[...] = cells.T.astype(BF16)
    sums[...] = jnp.broadcast_to(jnp.sum(cells, axis=1, keepdims=True), (RANK, LANES))
    gene_block(
        1 - info[AT_CORE], counts_ref, cell_copy, cell_turned, sums, half_of(info, gene_refs, False), out_ref
    )


def gene_second_kernel(info, counts_ref, cell_copy, cell_turned, sums, *refs):
    gene_block(
        info[AT_CORE], counts_ref, cell_copy, cell_turned, sums, half_of(info, refs[:-1], True), refs[-1]
    )


def gene_half(info, counts, left, genes):
    first = len(left) == 1
    n_cells, n_genes = counts.shape
    half = n_genes // CORES
    sums = struct((GROUPS, 8, half + LANES))
    made = [struct((RANK, n_cells), BF16), struct((n_cells, RANK), BF16), struct((RANK, LANES))]
    return kernel_call(
        gene_first_kernel if first else gene_second_kernel,
        info,
        (counts, *left, *genes),
        [sums] + made if first else [sums],
        vmem=PASS_VMEM,
        cost=pass_cost(n_cells, half),
    )


def cell_kernel(info, counts_ref, cells_ref, mine_ref, other_ref, out_ref, ordered, gene_copy):
    n_cells, n_genes = counts_ref.shape
    half = n_genes // CORES
    for side, ref in ((info[AT_CORE], mine_ref), (1 - info[AT_CORE], other_ref)):
        ordered[:, :, pl.ds(pl.multiple_of(side * half, half), half)] = ref[...]
    factor = ordered[...].reshape(RANK, n_genes)
    gene_copy[...] = factor.astype(BF16)
    sums = jnp.broadcast_to(jnp.sum(factor, axis=1, keepdims=True), (RANK, LANES))
    out_ref[:, :, n_cells:] = sums.reshape(GROUPS, 8, LANES)

    @pl.loop(0, n_cells // HIGH)
    def _(i):
        at = pl.multiple_of(i * HIGH, HIGH)
        rows = pl.ds(at, HIGH)
        cells = cells_ref[:, :, rows].reshape(RANK, HIGH).T.astype(BF16)
        numer = jnp.zeros((RANK, HIGH), F32)
        for start in range(0, n_genes, HIGH):
            cols = slice(start, start + HIGH)
            genes = gene_copy[:, cols]
            approx = jnp.dot(cells, genes, preferred_element_type=F32)
            ratio = ratio_of(counts_ref[rows, cols], approx)
            numer = numer + lax.dot_general(genes, ratio, (((1,), (1,)), ((), ())), preferred_element_type=F32)
        out_ref[:, :, rows] = numer.reshape(GROUPS, 8, HIGH)


def cell_pass(info, counts, cells, mine, other):
    n_cells, n_genes = counts.shape
    return kernel_call(
        cell_kernel,
        info,
        (counts, cells, mine, other),
        struct((GROUPS, 8, n_cells + LANES)),
        [pltpu.VMEM((GROUPS, 8, n_genes), F32), pltpu.VMEM((RANK, n_genes), BF16)],
        vmem=PASS_VMEM,
        cost=pass_cost(n_cells, n_genes),
    )


def pair_sum_kernel(info, a_ref, b_ref, out_ref):
    out_ref[...] = a_ref[...] + b_ref[...]


def spread_sum_kernel(info, parts_ref, out_ref):
    total = parts_ref[0]
    for i in range(1, parts_ref.shape[0]):
        total = total + parts_ref[i]
    for i in range(out_ref.shape[0]):
        out_ref[i] = total


def sum_kernel(info, parts_ref, out_ref):
    total = parts_ref[0]
    for i in range(1, parts_ref.shape[0]):
        total = total + parts_ref[i]
    out_ref[...] = total


def put_updated(piece, total, out_ref):
    width = piece.shape[1]
    new = piece * total[:, :width] / total[:, width : width + 1]
    for i in range(out_ref.shape[0]):
        out_ref[i] = new


def gene_update_kernel(info, parts_ref, *refs):
    total = parts_ref[0]
    for i in range(1, parts_ref.shape[0]):
        total = total + parts_ref[i]
    put_updated(half_of(info, refs[:-1], True)[info[AT_Y]], total, refs[-1])


def cell_update_kernel(info, cells_ref, *refs):
    total = refs[0][...]
    for ref in refs[1:-1]:
        total = total + ref[...]
    put_updated(cells_ref[info[AT_X]], total, refs[-1])


def join_genes_kernel(info, mine_ref, other_ref, out_ref):
    half = mine_ref.shape[2]
    for side, ref in ((info[AT_CORE], mine_ref), (1 - info[AT_CORE], other_ref)):
        out_ref[:, :, pl.ds(pl.multiple_of(side * half, half), half)] = ref[...]


def swap(a, axis):
    return lax.all_to_all(a, axis, 0, 0, tiled=True)


def per_device(n_z, n_zhi, counts, cell_factor, gene_factor):
    n_cells, n_genes = counts.shape
    half = n_genes // CORES
    info = jnp.stack([lax.axis_index(a) for a in ("core", "y", "x")]).astype(jnp.int32)
    to_core = lambda a: lax.ppermute(a, "core", [(0, 1), (1, 0)])
    to_zhi = lambda a, s: lax.ppermute(a, "z_hi", [(i, (i + s) % n_zhi) for i in range(n_zhi)])

    cells = cell_factor.reshape(GROUPS, 8, n_cells)
    genes = [gene_factor.reshape(GROUPS, 8, n_genes)]
    wide, long = half + LANES, n_cells + LANES
    for step in range(ITERS):
        sent, *left = gene_half(info, counts, [cells], genes)
        got = to_core(sent)
        kept = gene_half(info, counts, left, genes)[0]
        both = kernel_call(pair_sum_kernel, info, (kept, got), struct((Y, 8, wide)))
        part = kernel_call(spread_sum_kernel, info, (swap(both, "y"),), struct((n_z, 8, wide)))
        mine = kernel_call(gene_update_kernel, info, (swap(part, "z"), *genes), struct((Y, 8, half)))
        mine = swap(mine, "y")
        genes = [mine, to_core(mine)]

        sums = cell_pass(info, counts, cells, *genes)
        part = kernel_call(sum_kernel, info, (swap(sums, "x"),), struct((8, long)))
        got = [to_zhi(part, s) for s in range(1, n_zhi)]
        cells = kernel_call(cell_update_kernel, info, (cells, part, *got), struct((X, 8, n_cells)))
        cells = swap(cells, "x")
    joined = kernel_call(join_genes_kernel, info, genes, struct((GROUPS, 8, n_genes)))
    return cells.reshape(RANK, n_cells), joined.reshape(RANK, n_genes)


def solution(mesh):
    n_z, n_zhi = mesh.shape["cell"] // (Y * CORES), mesh.shape["gene"] // X
    cut = Mesh(mesh.devices.reshape(n_z, Y, CORES, n_zhi, X), ("z", "y", "core", "z_hi", "x"))
    cell, gene = ("z", "y", "core"), ("z_hi", "x")
    return jax.shard_map(
        functools.partial(per_device, n_z, n_zhi),
        mesh=cut,
        in_specs=(P(cell, gene), P(None, cell), P(None, gene)),
        out_specs=(P(None, cell), P(None, gene)),
        check_vma=False,
    )
```

```python
import functools

import jax
import jax.numpy as jnp
from jax import lax
from jax.experimental import pallas as pl
from jax.experimental.pallas import tpu as pltpu
from jax.sharding import Mesh
from jax.sharding import PartitionSpec as P

ITERS = 3
RANK = 32
GROUPS = 4
LANES = 128
TILE, WIDE, HIGH = 256, 1024, 512
CORES, Y, X = 2, 4, 4
SMALL_VMEM, PASS_VMEM = 4 << 20, 28 << 20
F32, BF16 = jnp.float32, jnp.bfloat16

AT_CORE, AT_Y, AT_Z, AT_X = range(4)


def struct(shape, dtype=F32):
    return jax.ShapeDtypeStruct(shape, dtype)


def kernel_call(kernel, info, operands, out_shape, scratch=(), vmem=SMALL_VMEM, cost=None):
    return pl.pallas_call(
        kernel,
        grid_spec=pltpu.PrefetchScalarGridSpec(
            num_scalar_prefetch=1,
            grid=(),
            in_specs=[pl.BlockSpec(memory_space=pltpu.VMEM)] * len(operands),
            out_specs=jax.tree.map(lambda _: pl.BlockSpec(memory_space=pltpu.VMEM), out_shape),
            scratch_shapes=list(scratch),
        ),
        out_shape=out_shape,
        compiler_params=pltpu.CompilerParams(vmem_limit_bytes=vmem),
        cost_estimate=cost,
    )(info, *operands)


def pass_cost(cells, genes):
    return pl.CostEstimate(flops=cells, bytes_accessed=genes, transcendentals=0)


def ratio_of(counts, approx):
    return (counts.astype(F32) * pl.reciprocal(approx, approx=True)).astype(BF16)


def span(index, size):
    return pl.ds(pl.multiple_of(index * size, size), size)


def fill_genes(refs, side, groups):
    (ref,) = refs
    half = groups.shape[2]
    if ref.shape[0] == GROUPS:
        groups[...] = ref[:, :, span(side, half)]
        return
    width = ref.shape[2]
    n_z = half // width
    for y in range(Y):
        for z in range(n_z):
            groups[y, :, z * width : (z + 1) * width] = ref[y * n_z + z]


def fill_cells(info, refs, whole):
    if len(refs) == 1:
        whole[...] = refs[0][...]
        return
    for s, ref in enumerate(refs):
        whole[:, span(lax.rem(info[AT_X] + (X - s), X), ref.shape[1])] = ref[...]


def gene_block(side, counts_ref, cell_copy, cell_turned, sums, groups, out_ref):
    n_cells = counts_ref.shape[0]
    half = out_ref.shape[2] - LANES
    base = side * half

    @pl.loop(0, half // WIDE)
    def _(j):
        at = pl.multiple_of(j * WIDE, WIDE)
        cols = pl.ds(pl.multiple_of(base + at, WIDE), WIDE)
        genes = groups[:, :, pl.ds(at, WIDE)].reshape(RANK, WIDE).astype(BF16)
        numer = jnp.zeros((RANK, WIDE), F32)
        for start in range(0, n_cells, TILE):
            rows = slice(start, start + TILE)
            approx = jnp.dot(cell_turned[rows, :], genes, preferred_element_type=F32)
            ratio = ratio_of(counts_ref[rows, cols], approx)
            numer = numer + jnp.dot(cell_copy[:, rows], ratio, preferred_element_type=F32)
        out_ref[:, :, pl.ds(at, WIDE)] = numer.reshape(GROUPS, 8, WIDE)

    out_ref[:, :, half:] = sums[...].reshape(GROUPS, 8, LANES)


def gene_first_kernel(n_cell_refs, info, counts_ref, *refs):
    cell_refs, gene_refs = refs[:n_cell_refs], refs[n_cell_refs:-6]
    out_ref, cell_copy, cell_turned, sums, whole, groups = refs[-6:]
    fill_cells(info, cell_refs, whole)
    cells = whole[...]
    cell_copy[...] = cells.astype(BF16)
    cell_turned[...] = cells.T.astype(BF16)
    sums[...] = jnp.broadcast_to(jnp.sum(cells, axis=1, keepdims=True), (RANK, LANES))
    fill_genes(gene_refs, 1 - info[AT_CORE], groups)
    gene_block(1 - info[AT_CORE], counts_ref, cell_copy, cell_turned, sums, groups, out_ref)


def gene_second_kernel(info, counts_ref, cell_copy, cell_turned, sums, gene_ref, out_ref, groups):
    fill_genes([gene_ref], info[AT_CORE], groups)
    gene_block(info[AT_CORE], counts_ref, cell_copy, cell_turned, sums, groups, out_ref)


def gene_first(info, counts, cells, genes):
    n_cells, n_genes = counts.shape
    half = n_genes // CORES
    return kernel_call(
        functools.partial(gene_first_kernel, len(cells)),
        info,
        (counts, *cells, genes),
        [
            struct((GROUPS, 8, half + LANES)),
            struct((RANK, n_cells), BF16),
            struct((n_cells, RANK), BF16),
            struct((RANK, LANES)),
        ],
        [pltpu.VMEM((RANK, n_cells), F32), pltpu.VMEM((GROUPS, 8, half), F32)],
        vmem=PASS_VMEM,
        cost=pass_cost(n_cells, half),
    )


def gene_second(info, counts, left, genes):
    n_cells, n_genes = counts.shape
    half = n_genes // CORES
    return kernel_call(
        gene_second_kernel,
        info,
        (counts, *left, genes),
        struct((GROUPS, 8, half + LANES)),
        [pltpu.VMEM((GROUPS, 8, half), F32)],
        vmem=PASS_VMEM,
        cost=pass_cost(n_cells, half),
    )


def cell_block(to, info, counts_ref, cell_turned, gene_copy, sums, out_ref):
    n_genes = counts_ref.shape[1]
    quarter = out_ref.shape[1] - LANES
    rows = span(lax.rem(info[AT_X] + to, X), quarter)
    out_ref[:, quarter:] = sums[...]
    cells = cell_turned[rows, :]
    numer = jnp.zeros((RANK, quarter), F32)
    for start in range(0, n_genes, HIGH):
        cols = slice(start, start + HIGH)
        genes = gene_copy[:, cols]
        approx = jnp.dot(cells, genes, preferred_element_type=F32)
        ratio = ratio_of(counts_ref[rows, cols], approx)
        numer = numer + lax.dot_general(genes, ratio, (((1,), (1,)), ((), ())), preferred_element_type=F32)
    out_ref[:, :quarter] = numer


def cell_first_kernel(to, info, counts_ref, cell_turned, mine_ref, other_ref, out_ref, gene_copy, sums, ordered):
    half = ordered.shape[2] // CORES
    for side, ref in ((info[AT_CORE], mine_ref), (1 - info[AT_CORE], other_ref)):
        fill_genes([ref], side, ordered.at[:, :, span(side, half)])
    factor = ordered[...].reshape(RANK, CORES * half)
    gene_copy[...] = factor.astype(BF16)
    sums[...] = jnp.broadcast_to(jnp.sum(factor, axis=1, keepdims=True), (RANK, LANES))
    cell_block(to, info, counts_ref, cell_turned, gene_copy, sums, out_ref)


def cell_quarter(info, counts, to, cell_turned, left, first):
    n_cells, n_genes = counts.shape
    quarter = n_cells // X
    sums = struct((RANK, quarter + LANES))
    made = [struct((RANK, n_genes), BF16), struct((RANK, LANES))]
    return kernel_call(
        functools.partial(cell_first_kernel if first else cell_block, to),
        info,
        (counts, cell_turned, *left),
        [sums] + made if first else [sums],
        [pltpu.VMEM((GROUPS, 8, n_genes), F32)] if first else [],
        vmem=PASS_VMEM,
        cost=pass_cost(quarter, n_genes),
    )


def pair_sum_kernel(info, a_ref, b_ref, out_ref):
    width = out_ref.shape[2] - LANES
    half = a_ref.shape[2] - LANES
    n_z = half // width
    for y in range(Y):
        total = a_ref[y] + b_ref[y]
        for z in range(n_z):
            out_ref[y * n_z + z, :, :width] = total[:, z * width : (z + 1) * width]
            out_ref[y * n_z + z, :, width:] = total[:, half:]


def four_sum_kernel(info, a_ref, b_ref, c_ref, d_ref, out_ref):
    out_ref[...] = (a_ref[...] + b_ref[...]) + (c_ref[...] + d_ref[...])


def updated(piece, total):
    width = piece.shape[1]
    return piece * total[:, :width] / total[:, width : width + 1]


def gene_update_kernel(info, parts_ref, old_ref, new_ref, spread_ref):
    total = parts_ref[0]
    for i in range(1, parts_ref.shape[0]):
        total = total + parts_ref[i]
    width = new_ref.shape[1]
    if old_ref.ndim == 2:
        old = old_ref[...]
    else:
        n_z = parts_ref.shape[0] // Y
        old = old_ref[info[AT_Y], :, span(info[AT_CORE] * n_z + info[AT_Z], width)]
    new = updated(old, total)
    new_ref[...] = new
    for i in range(spread_ref.shape[0]):
        spread_ref[i] = new


def cell_update_kernel(info, old_ref, *refs):
    total = refs[0][...]
    for ref in refs[1:-1]:
        total = total + ref[...]
    width = refs[-1].shape[1]
    old = old_ref[...] if old_ref.shape[1] == width else old_ref[:, span(info[AT_X], width)]
    refs[-1][...] = updated(old, total)


def join_genes_kernel(info, mine_ref, other_ref, out_ref):
    half = out_ref.shape[2] // CORES
    for side, ref in ((info[AT_CORE], mine_ref), (1 - info[AT_CORE], other_ref)):
        fill_genes([ref], side, out_ref.at[:, :, span(side, half)])


def join_cells_kernel(info, *refs):
    fill_cells(info, refs[:-1], refs[-1])


def per_device(n_z, n_zhi, counts, cell_factor, gene_factor):
    n_cells, n_genes = counts.shape
    half, quarter, width = n_genes // CORES, n_cells // X, n_genes // (CORES * n_z)
    info = jnp.stack([lax.axis_index(a) for a in ("core", "y", "z", "x")]).astype(jnp.int32)
    swap = lambda a: lax.all_to_all(a, ("y", "z"), 0, 0, tiled=True)
    shift = lambda a, axis, n, s: lax.ppermute(a, axis, [(i, (i + s) % n) for i in range(n)])

    cells = [cell_factor]
    mine = other = piece = gene_factor.reshape(GROUPS, 8, n_genes)
    for step in range(ITERS):
        sent, *left = gene_first(info, counts, cells, other)
        got = shift(sent, "core", CORES, 1)
        kept = gene_second(info, counts, left, mine)
        parts = kernel_call(pair_sum_kernel, info, (kept, got), struct((Y * n_z, 8, width + LANES)))
        piece, spread = kernel_call(
            gene_update_kernel, info, (swap(parts), piece), [struct((8, width)), struct((Y * n_z, 8, width))]
        )
        mine = swap(spread)
        other = shift(mine, "core", CORES, 1)

        cell_turned, left = left[1], (mine, other)
        got = {}
        for s in (2, 1, 3, 0):
            sums, *made = cell_quarter(info, counts, s, cell_turned, left, not got)
            sums, left = lax.optimization_barrier((sums, made or left))
            got[s] = shift(sums, "x", X, s) if s else sums
        part = kernel_call(four_sum_kernel, info, [got[s] for s in range(X)], struct((RANK, quarter + LANES)))
        got = [shift(part, "z_hi", n_zhi, s) for s in range(1, n_zhi)]
        new = kernel_call(cell_update_kernel, info, (cells[0], part, *got), struct((RANK, quarter)))
        cells = [new] + [shift(new, "x", X, s) for s in (1, 2, 3)]
    joined = kernel_call(join_genes_kernel, info, (mine, other), struct((GROUPS, 8, n_genes)))
    cells = kernel_call(join_cells_kernel, info, cells, struct((RANK, n_cells)))
    return cells, joined.reshape(RANK, n_genes)


def solution(mesh):
    n_z, n_zhi = mesh.shape["cell"] // (Y * CORES), mesh.shape["gene"] // X
    cut = Mesh(mesh.devices.reshape(n_z, Y, CORES, n_zhi, X), ("z", "y", "core", "z_hi", "x"))
    cell, gene = ("z", "y", "core"), ("z_hi", "x")
    return jax.shard_map(
        functools.partial(per_device, n_z, n_zhi),
        mesh=cut,
        in_specs=(P(cell, gene), P(None, cell), P(None, gene)),
        out_specs=(P(None, cell), P(None, gene)),
        check_vma=False,
    )
```

```python
import functools

import jax
import jax.numpy as jnp
from jax import lax
from jax.experimental import pallas as pl
from jax.experimental.pallas import tpu as pltpu
from jax.sharding import Mesh
from jax.sharding import PartitionSpec as P

ITERS = 3
RANK = 32
GROUPS = 4
LANES = 128
WIDE = 1024
CORES, Y, X = 2, 4, 4
SMALL_VMEM, PASS_VMEM = 4 << 20, 28 << 20
F32, BF16 = jnp.float32, jnp.bfloat16

AT_CORE, AT_Y, AT_Z, AT_X = range(4)


def struct(shape, dtype=F32):
    return jax.ShapeDtypeStruct(shape, dtype)


def kernel_call(kernel, info, operands, out_shape, scratch=(), vmem=SMALL_VMEM, cost=None):
    return pl.pallas_call(
        kernel,
        grid_spec=pltpu.PrefetchScalarGridSpec(
            num_scalar_prefetch=1,
            grid=(),
            in_specs=[pl.BlockSpec(memory_space=pltpu.VMEM)] * len(operands),
            out_specs=jax.tree.map(lambda _: pl.BlockSpec(memory_space=pltpu.VMEM), out_shape),
            scratch_shapes=list(scratch),
        ),
        out_shape=out_shape,
        compiler_params=pltpu.CompilerParams(vmem_limit_bytes=vmem),
        cost_estimate=cost,
    )(info, *operands)


def pass_cost(cells, genes):
    return pl.CostEstimate(flops=cells, bytes_accessed=genes, transcendentals=0)


def ratio_of(counts, approx):
    return (counts.astype(F32) * pl.reciprocal(approx, approx=True)).astype(BF16)


def span(index, size):
    return pl.ds(pl.multiple_of(index * size, size), size)


def fill_genes(refs, side, groups):
    (ref,) = refs
    half = groups.shape[2]
    if ref.shape[0] == GROUPS:
        groups[...] = ref[:, :, span(side, half)]
        return
    width = ref.shape[2]
    n_z = half // width
    for y in range(Y):
        for z in range(n_z):
            groups[y, :, z * width : (z + 1) * width] = ref[y * n_z + z]


def gene_block(counts_ref, rows, cols, turned, copy, genes):
    approx = jnp.dot(turned, genes, preferred_element_type=F32)
    ratio = ratio_of(counts_ref[rows, cols], approx)
    return jnp.dot(copy, ratio, preferred_element_type=F32)


def gene_own(info, counts_ref, piece, gene_copy, out_ref):
    n_genes = counts_ref.shape[1]
    rows = span(info[AT_X], piece.shape[1])
    copy, turned = piece.astype(BF16), piece.T.astype(BF16)
    for start in range(0, n_genes, WIDE):
        cols = slice(start, start + WIDE)
        out_ref[:, cols] = gene_block(counts_ref, rows, cols, turned, copy, gene_copy[:, cols])


def gene_start_kernel(info, counts_ref, cells_ref, genes_ref, out_ref, gene_copy, *piece_refs):
    for s, ref in enumerate(piece_refs):
        ref[...] = cells_ref[:, span(lax.rem(info[AT_X] + (X - s), X), ref.shape[1])]
    gene_copy[...] = genes_ref[...].reshape(RANK, counts_ref.shape[1]).astype(BF16)
    gene_own(info, counts_ref, piece_refs[0][...], gene_copy, out_ref)


def gene_own_kernel(info, counts_ref, piece_ref, gene_copy, out_ref):
    gene_own(info, counts_ref, piece_ref[...], gene_copy, out_ref)


def gene_half(side, info, counts_ref, begun_ref, gene_copy, cell_copy, cell_turned, sums, out_ref):
    half = out_ref.shape[2] - LANES
    quarter = counts_ref.shape[0] // X
    cols = span(side, half)
    genes = gene_copy[:, cols]
    numer = begun_ref[:, cols]
    for s in range(1, X):
        rows = span(lax.rem(info[AT_X] + (X - s), X), quarter)
        part = slice(s * quarter, (s + 1) * quarter)
        numer = numer + gene_block(counts_ref, rows, cols, cell_turned[part, :], cell_copy[:, part], genes)
    out_ref[:, :, :half] = numer.reshape(GROUPS, 8, half)
    out_ref[:, :, half:] = sums[...].reshape(GROUPS, 8, LANES)


def gene_first_kernel(info, counts_ref, begun_ref, gene_copy, f0, f1, f2, f3, out_ref, cell_copy, cell_turned, sums):
    total = jnp.zeros((RANK, 1), F32)
    for s, ref in enumerate((f0, f1, f2, f3)):
        piece = ref[...]
        part = slice(s * piece.shape[1], (s + 1) * piece.shape[1])
        cell_copy[:, part] = piece.astype(BF16)
        cell_turned[part, :] = piece.T.astype(BF16)
        total = total + jnp.sum(piece, axis=1, keepdims=True)
    sums[...] = jnp.broadcast_to(total, (RANK, LANES))
    gene_half(1 - info[AT_CORE], info, counts_ref, begun_ref, gene_copy, cell_copy, cell_turned, sums, out_ref)


def gene_second_kernel(info, counts_ref, begun_ref, gene_copy, cell_copy, cell_turned, sums, out_ref):
    gene_half(info[AT_CORE], info, counts_ref, begun_ref, gene_copy, cell_copy, cell_turned, sums, out_ref)


def pass_call(kernel, info, operands, out_shape, cells, genes, scratch=()):
    return kernel_call(kernel, info, operands, out_shape, scratch, PASS_VMEM, pass_cost(cells, genes))


def gene_pass(info, counts, begun, gene_copy, cells):
    n_cells, n_genes = counts.shape
    half = n_genes // CORES
    out = struct((GROUPS, 8, half + LANES))
    made = [struct((RANK, n_cells), BF16), struct((n_cells, RANK), BF16), struct((RANK, LANES))]
    sent, *made = pass_call(gene_first_kernel, info, (counts, begun, gene_copy, *cells), [out] + made, n_cells, half)
    own = lambda: pass_call(gene_second_kernel, info, (counts, begun, gene_copy, *made), out, n_cells, half)
    return sent, made[1], own


def cell_block(to, info, counts_ref, cell_turned, gene_copy, sums, out_ref):
    n_genes = counts_ref.shape[1]
    quarter = out_ref.shape[1] - LANES
    rows = span(lax.rem(info[AT_X] + to, X), quarter)
    at = (X - to) % X * quarter
    out_ref[:, quarter:] = sums[...]
    cells = cell_turned[at : at + quarter, :]
    numer = jnp.zeros((RANK, quarter), F32)
    for start in range(0, n_genes, WIDE):
        cols = slice(start, start + WIDE)
        genes = gene_copy[:, cols]
        approx = jnp.dot(cells, genes, preferred_element_type=F32)
        ratio = ratio_of(counts_ref[rows, cols], approx)
        numer = numer + lax.dot_general(genes, ratio, (((1,), (1,)), ((), ())), preferred_element_type=F32)
    out_ref[:, :quarter] = numer


def cell_first_kernel(to, info, counts_ref, cell_turned, mine_ref, other_ref, out_ref, gene_copy, sums, ordered):
    half = ordered.shape[2] // CORES
    for side, ref in ((info[AT_CORE], mine_ref), (1 - info[AT_CORE], other_ref)):
        fill_genes([ref], side, ordered.at[:, :, span(side, half)])
    factor = ordered[...].reshape(RANK, CORES * half)
    gene_copy[...] = factor.astype(BF16)
    sums[...] = jnp.broadcast_to(jnp.sum(factor, axis=1, keepdims=True), (RANK, LANES))
    cell_block(to, info, counts_ref, cell_turned, gene_copy, sums, out_ref)


def cell_quarter(info, counts, to, cell_turned, left, first):
    n_cells, n_genes = counts.shape
    quarter = n_cells // X
    sums = struct((RANK, quarter + LANES))
    made = [struct((RANK, n_genes), BF16), struct((RANK, LANES))]
    return kernel_call(
        functools.partial(cell_first_kernel if first else cell_block, to),
        info,
        (counts, cell_turned, *left),
        [sums] + made if first else [sums],
        [pltpu.VMEM((GROUPS, 8, n_genes), F32)] if first else [],
        vmem=PASS_VMEM,
        cost=pass_cost(quarter, n_genes),
    )


def pair_sum_kernel(info, a_ref, b_ref, out_ref):
    width = out_ref.shape[2] - LANES
    half = a_ref.shape[2] - LANES
    n_z = half // width
    for y in range(Y):
        total = a_ref[y] + b_ref[y]
        for z in range(n_z):
            out_ref[y * n_z + z, :, :width] = total[:, z * width : (z + 1) * width]
            out_ref[y * n_z + z, :, width:] = total[:, half:]


def four_sum_kernel(info, a_ref, b_ref, c_ref, d_ref, out_ref):
    out_ref[...] = (a_ref[...] + b_ref[...]) + (c_ref[...] + d_ref[...])


def updated(piece, total):
    width = piece.shape[1]
    return piece * total[:, :width] / total[:, width : width + 1]


def gene_update_kernel(info, parts_ref, old_ref, new_ref, spread_ref):
    total = parts_ref[0]
    for i in range(1, parts_ref.shape[0]):
        total = total + parts_ref[i]
    width = new_ref.shape[1]
    if old_ref.ndim == 2:
        old = old_ref[...]
    else:
        n_z = parts_ref.shape[0] // Y
        old = old_ref[info[AT_Y], :, span(info[AT_CORE] * n_z + info[AT_Z], width)]
    new = updated(old, total)
    new_ref[...] = new
    for i in range(spread_ref.shape[0]):
        spread_ref[i] = new


def cell_update_kernel(info, old_ref, *refs):
    total = refs[0][...]
    for ref in refs[1:-1]:
        total = total + ref[...]
    refs[-1][...] = updated(old_ref[...], total)


def join_genes_kernel(info, mine_ref, other_ref, out_ref):
    half = out_ref.shape[2] // CORES
    for side, ref in ((info[AT_CORE], mine_ref), (1 - info[AT_CORE], other_ref)):
        fill_genes([ref], side, out_ref.at[:, :, span(side, half)])


def join_cells_kernel(info, *refs):
    for s, ref in enumerate(refs[:-1]):
        refs[-1][:, span(lax.rem(info[AT_X] + (X - s), X), ref.shape[1])] = ref[...]


def per_device(n_z, n_zhi, counts, cell_factor, gene_factor):
    n_cells, n_genes = counts.shape
    half, quarter, width = n_genes // CORES, n_cells // X, n_genes // (CORES * n_z)
    info = jnp.stack([lax.axis_index(a) for a in ("core", "y", "z", "x")]).astype(jnp.int32)
    swap = lambda a: lax.all_to_all(a, ("y", "z"), 0, 0, tiled=True)
    shift = lambda a, axis, n, s: lax.ppermute(a, axis, [(i, (i + s) % n) for i in range(n)])

    piece = gene_factor.reshape(GROUPS, 8, n_genes)
    begun, gene_copy, *cells = pass_call(
        gene_start_kernel,
        info,
        (counts, cell_factor, piece),
        [struct((RANK, n_genes)), struct((RANK, n_genes), BF16)] + [struct((RANK, quarter))] * X,
        quarter,
        n_genes,
    )
    for step in range(ITERS):
        if step:
            begun = pass_call(
                gene_own_kernel, info, (counts, cells[0], gene_copy), struct((RANK, n_genes)), quarter, n_genes
            )
        sent, cell_turned, own = gene_pass(info, counts, begun, gene_copy, cells)
        got = shift(sent, "core", CORES, 1)
        kept = own()
        parts = kernel_call(pair_sum_kernel, info, (kept, got), struct((Y * n_z, 8, width + LANES)))
        piece, spread = kernel_call(
            gene_update_kernel, info, (swap(parts), piece), [struct((8, width)), struct((Y * n_z, 8, width))]
        )
        mine = swap(spread)
        other = shift(mine, "core", CORES, 1)

        left = (mine, other)
        got = {}
        for s in (2, 1, 3, 0):
            sums, *made = cell_quarter(info, counts, s, cell_turned, left, not got)
            sums, left = lax.optimization_barrier((sums, made or left))
            got[s] = shift(sums, "x", X, s) if s else sums
        gene_copy = left[0]
        part = kernel_call(four_sum_kernel, info, [got[s] for s in range(X)], struct((RANK, quarter + LANES)))
        got = [shift(part, "z_hi", n_zhi, s) for s in range(1, n_zhi)]
        new = kernel_call(cell_update_kernel, info, (cells[0], part, *got), struct((RANK, quarter)))
        cells = [new] + [shift(new, "x", X, s) for s in (1, 2, 3)]
    joined = kernel_call(join_genes_kernel, info, (mine, other), struct((GROUPS, 8, n_genes)))
    cells = kernel_call(join_cells_kernel, info, cells, struct((RANK, n_cells)))
    return cells, joined.reshape(RANK, n_genes)


def solution(mesh):
    n_z, n_zhi = mesh.shape["cell"] // (Y * CORES), mesh.shape["gene"] // X
    cut = Mesh(mesh.devices.reshape(n_z, Y, CORES, n_zhi, X), ("z", "y", "core", "z_hi", "x"))
    cell, gene = ("z", "y", "core"), ("z_hi", "x")
    return jax.shard_map(
        functools.partial(per_device, n_z, n_zhi),
        mesh=cut,
        in_specs=(P(cell, gene), P(None, cell), P(None, gene)),
        out_specs=(P(None, cell), P(None, gene)),
        check_vma=False,
    )
```

```python
import functools

import jax
import jax.numpy as jnp
from jax import lax
from jax.experimental import pallas as pl
from jax.experimental.pallas import tpu as pltpu
from jax.sharding import Mesh
from jax.sharding import PartitionSpec as P

ITERS = 3
RANK = 32
GROUPS = 4
LANES = 128
WIDE = 1024
CORES, Y, X = 2, 4, 4
SMALL_VMEM, PASS_VMEM = 4 << 20, 28 << 20
F32, BF16 = jnp.float32, jnp.bfloat16

AT_CORE, AT_Y, AT_Z, AT_X = range(4)


def struct(shape, dtype=F32):
    return jax.ShapeDtypeStruct(shape, dtype)


def kernel_call(kernel, info, operands, out_shape, scratch=(), vmem=SMALL_VMEM, cost=None):
    return pl.pallas_call(
        kernel,
        grid_spec=pltpu.PrefetchScalarGridSpec(
            num_scalar_prefetch=1,
            grid=(),
            in_specs=[pl.BlockSpec(memory_space=pltpu.VMEM)] * len(operands),
            out_specs=jax.tree.map(lambda _: pl.BlockSpec(memory_space=pltpu.VMEM), out_shape),
            scratch_shapes=list(scratch),
        ),
        out_shape=out_shape,
        compiler_params=pltpu.CompilerParams(vmem_limit_bytes=vmem),
        cost_estimate=cost,
    )(info, *operands)


def pass_cost(cells, genes):
    return pl.CostEstimate(flops=cells, bytes_accessed=genes, transcendentals=0)


def ratio_of(counts, approx):
    return (counts.astype(F32) * pl.reciprocal(approx, approx=True)).astype(BF16)


def span(index, size):
    return pl.ds(pl.multiple_of(index * size, size), size)


def fill_genes(refs, side, groups):
    (ref,) = refs
    half = groups.shape[2]
    if ref.shape[0] == GROUPS:
        groups[...] = ref[:, :, span(side, half)]
        return
    width = ref.shape[2]
    n_z = half // width
    for y in range(Y):
        for z in range(n_z):
            groups[y, :, z * width : (z + 1) * width] = ref[y * n_z + z]


def gene_block(counts_ref, rows, cols, turned, copy, genes):
    approx = jnp.dot(turned, genes, preferred_element_type=F32)
    ratio = ratio_of(counts_ref[rows, cols], approx)
    return jnp.dot(copy, ratio, preferred_element_type=F32)


def gene_quarter(s, info, counts_ref, piece, gene_copy, out_ref, begun_ref=None):
    n_genes = counts_ref.shape[1]
    rows = span(lax.rem(info[AT_X] + (X - s), X), piece.shape[1])
    copy, turned = piece.astype(BF16), piece.T.astype(BF16)
    for start in range(0, n_genes, WIDE):
        cols = slice(start, start + WIDE)
        numer = gene_block(counts_ref, rows, cols, turned, copy, gene_copy[:, cols])
        out_ref[:, cols] = numer if begun_ref is None else begun_ref[:, cols] + numer


def gene_start_kernel(info, counts_ref, cells_ref, genes_ref, out_ref, gene_copy, *piece_refs):
    for s, ref in enumerate(piece_refs):
        ref[...] = cells_ref[:, span(lax.rem(info[AT_X] + (X - s), X), ref.shape[1])]
    gene_copy[...] = genes_ref[...].reshape(RANK, counts_ref.shape[1]).astype(BF16)
    gene_quarter(0, info, counts_ref, piece_refs[0][...], gene_copy, out_ref)


def gene_own_kernel(info, counts_ref, piece_ref, gene_copy, out_ref):
    gene_quarter(0, info, counts_ref, piece_ref[...], gene_copy, out_ref)


def gene_next_kernel(info, counts_ref, piece_ref, gene_copy, begun_ref, out_ref):
    gene_quarter(X - 1, info, counts_ref, piece_ref[...], gene_copy, out_ref, begun_ref)


def gene_half(side, info, counts_ref, begun_ref, gene_copy, cell_copy, cell_turned, sums, out_ref):
    half = out_ref.shape[2] - LANES
    quarter = counts_ref.shape[0] // X
    cols = span(side, half)
    genes = gene_copy[:, cols]
    numer = begun_ref[:, cols]
    for s in range(1, X - 1):
        rows = span(lax.rem(info[AT_X] + (X - s), X), quarter)
        part = slice(s * quarter, (s + 1) * quarter)
        numer = numer + gene_block(counts_ref, rows, cols, cell_turned[part, :], cell_copy[:, part], genes)
    out_ref[:, :, :half] = numer.reshape(GROUPS, 8, half)
    out_ref[:, :, half:] = sums[...].reshape(GROUPS, 8, LANES)


def gene_first_kernel(info, counts_ref, begun_ref, gene_copy, f0, f1, f2, f3, out_ref, cell_copy, cell_turned, sums):
    total = jnp.zeros((RANK, 1), F32)
    for s, ref in enumerate((f0, f1, f2, f3)):
        piece = ref[...]
        part = slice(s * piece.shape[1], (s + 1) * piece.shape[1])
        cell_copy[:, part] = piece.astype(BF16)
        cell_turned[part, :] = piece.T.astype(BF16)
        total = total + jnp.sum(piece, axis=1, keepdims=True)
    sums[...] = jnp.broadcast_to(total, (RANK, LANES))
    gene_half(1 - info[AT_CORE], info, counts_ref, begun_ref, gene_copy, cell_copy, cell_turned, sums, out_ref)


def gene_second_kernel(info, counts_ref, begun_ref, gene_copy, cell_copy, cell_turned, sums, out_ref):
    gene_half(info[AT_CORE], info, counts_ref, begun_ref, gene_copy, cell_copy, cell_turned, sums, out_ref)


def pass_call(kernel, info, operands, out_shape, cells, genes, scratch=()):
    return kernel_call(kernel, info, operands, out_shape, scratch, PASS_VMEM, pass_cost(cells, genes))


def gene_pass(info, counts, begun, gene_copy, cells):
    n_cells, n_genes = counts.shape
    half = n_genes // CORES
    out = struct((GROUPS, 8, half + LANES))
    made = [struct((RANK, n_cells), BF16), struct((n_cells, RANK), BF16), struct((RANK, LANES))]
    sent, *made = pass_call(gene_first_kernel, info, (counts, begun, gene_copy, *cells), [out] + made, n_cells, half)
    own = lambda: pass_call(gene_second_kernel, info, (counts, begun, gene_copy, *made), out, n_cells, half)
    return sent, made[1], own


def cell_rows(to, info, cell_turned, quarter):
    at = (X - to) % X * quarter
    return span(lax.rem(info[AT_X] + to, X), quarter), cell_turned[at : at + quarter, :]


def cell_block(counts_ref, rows, cols, cells, genes):
    approx = jnp.dot(cells, genes, preferred_element_type=F32)
    ratio = ratio_of(counts_ref[rows, cols], approx)
    return lax.dot_general(genes, ratio, (((1,), (1,)), ((), ())), preferred_element_type=F32)


def cell_begin_kernel(to, info, counts_ref, cell_turned, mine_ref, out_ref, groups):
    quarter, half = out_ref.shape[1], groups.shape[2]
    fill_genes([mine_ref], 0, groups)
    genes = groups[...].reshape(RANK, half).astype(BF16)
    rows, cells = cell_rows(to, info, cell_turned, quarter)
    out_ref[...] = cell_block(counts_ref, rows, span(info[AT_CORE], half), cells, genes)


def cell_first_kernel(
    to, info, counts_ref, cell_turned, begun_ref, mine_ref, other_ref, out_ref, gene_copy, sums, ordered
):
    half = ordered.shape[2] // CORES
    quarter = begun_ref.shape[1]
    for side, ref in ((info[AT_CORE], mine_ref), (1 - info[AT_CORE], other_ref)):
        fill_genes([ref], side, ordered.at[:, :, span(side, half)])
    factor = ordered[...].reshape(RANK, CORES * half)
    gene_copy[...] = factor.astype(BF16)
    sums[...] = jnp.broadcast_to(jnp.sum(factor, axis=1, keepdims=True), (RANK, LANES))
    rows, cells = cell_rows(to, info, cell_turned, quarter)
    cols = span(1 - info[AT_CORE], half)
    out_ref[:, :quarter] = begun_ref[...] + cell_block(counts_ref, rows, cols, cells, gene_copy[:, cols])
    out_ref[:, quarter:] = sums[...]


def cell_later_kernel(to, info, counts_ref, cell_turned, gene_copy, sums, out_ref):
    quarter = out_ref.shape[1] - LANES
    rows, cells = cell_rows(to, info, cell_turned, quarter)
    numer = jnp.zeros((RANK, quarter), F32)
    for start in range(0, counts_ref.shape[1], WIDE):
        cols = slice(start, start + WIDE)
        numer = numer + cell_block(counts_ref, rows, cols, cells, gene_copy[:, cols])
    out_ref[:, :quarter] = numer
    out_ref[:, quarter:] = sums[...]


def cell_begin(info, counts, to, cell_turned, mine):
    n_cells, n_genes = counts.shape
    return pass_call(
        functools.partial(cell_begin_kernel, to),
        info,
        (counts, cell_turned, mine),
        struct((RANK, n_cells // X)),
        n_cells // X,
        n_genes // CORES,
        [pltpu.VMEM((GROUPS, 8, n_genes // CORES), F32)],
    )


def cell_quarter(info, counts, to, cell_turned, left, first):
    n_cells, n_genes = counts.shape
    quarter = n_cells // X
    sums = struct((RANK, quarter + LANES))
    made = [struct((RANK, n_genes), BF16), struct((RANK, LANES))]
    return pass_call(
        functools.partial(cell_first_kernel if first else cell_later_kernel, to),
        info,
        (counts, cell_turned, *left),
        [sums] + made if first else [sums],
        quarter,
        n_genes,
        [pltpu.VMEM((GROUPS, 8, n_genes), F32)] if first else [],
    )


def pair_sum_kernel(info, a_ref, b_ref, out_ref):
    width = out_ref.shape[2] - LANES
    half = a_ref.shape[2] - LANES
    n_z = half // width
    for y in range(Y):
        total = a_ref[y] + b_ref[y]
        for z in range(n_z):
            out_ref[y * n_z + z, :, :width] = total[:, z * width : (z + 1) * width]
            out_ref[y * n_z + z, :, width:] = total[:, half:]


def four_sum_kernel(info, a_ref, b_ref, c_ref, d_ref, out_ref):
    out_ref[...] = (a_ref[...] + b_ref[...]) + (c_ref[...] + d_ref[...])


def updated(piece, total):
    width = piece.shape[1]
    return piece * total[:, :width] / total[:, width : width + 1]


def gene_update_kernel(info, parts_ref, old_ref, new_ref, spread_ref):
    total = parts_ref[0]
    for i in range(1, parts_ref.shape[0]):
        total = total + parts_ref[i]
    width = new_ref.shape[1]
    if old_ref.ndim == 2:
        old = old_ref[...]
    else:
        n_z = parts_ref.shape[0] // Y
        old = old_ref[info[AT_Y], :, span(info[AT_CORE] * n_z + info[AT_Z], width)]
    new = updated(old, total)
    new_ref[...] = new
    for i in range(spread_ref.shape[0]):
        spread_ref[i] = new


def cell_update_kernel(info, old_ref, *refs):
    total = refs[0][...]
    for ref in refs[1:-1]:
        total = total + ref[...]
    refs[-1][...] = updated(old_ref[...], total)


def join_genes_kernel(info, mine_ref, other_ref, out_ref):
    half = out_ref.shape[2] // CORES
    for side, ref in ((info[AT_CORE], mine_ref), (1 - info[AT_CORE], other_ref)):
        fill_genes([ref], side, out_ref.at[:, :, span(side, half)])


def join_cells_kernel(info, *refs):
    for s, ref in enumerate(refs[:-1]):
        refs[-1][:, span(lax.rem(info[AT_X] + (X - s), X), ref.shape[1])] = ref[...]


def per_device(n_z, n_zhi, counts, cell_factor, gene_factor):
    n_cells, n_genes = counts.shape
    half, quarter, width = n_genes // CORES, n_cells // X, n_genes // (CORES * n_z)
    info = jnp.stack([lax.axis_index(a) for a in ("core", "y", "z", "x")]).astype(jnp.int32)
    swap = lambda a: lax.all_to_all(a, ("y", "z"), 0, 0, tiled=True)
    shift = lambda a, axis, n, s: lax.ppermute(a, axis, [(i, (i + s) % n) for i in range(n)])

    piece = gene_factor.reshape(GROUPS, 8, n_genes)
    begun, gene_copy, *cells = pass_call(
        gene_start_kernel,
        info,
        (counts, cell_factor, piece),
        [struct((RANK, n_genes)), struct((RANK, n_genes), BF16)] + [struct((RANK, quarter))] * X,
        quarter,
        n_genes,
    )
    for step in range(ITERS):
        if step:
            begun = pass_call(
                gene_own_kernel, info, (counts, cells[0], gene_copy), struct((RANK, n_genes)), quarter, n_genes
            )
        begun = pass_call(
            gene_next_kernel,
            info,
            (counts, cells[X - 1], gene_copy, begun),
            struct((RANK, n_genes)),
            quarter,
            n_genes,
        )
        sent, cell_turned, own = gene_pass(info, counts, begun, gene_copy, cells)
        got = shift(sent, "core", CORES, 1)
        kept = own()
        parts = kernel_call(pair_sum_kernel, info, (kept, got), struct((Y * n_z, 8, width + LANES)))
        piece, spread = kernel_call(
            gene_update_kernel, info, (swap(parts), piece), [struct((8, width)), struct((Y * n_z, 8, width))]
        )
        mine = swap(spread)
        other = shift(mine, "core", CORES, 1)

        left = (cell_begin(info, counts, 2, cell_turned, mine), mine, other)
        got = {}
        for s in (2, 1, 3, 0):
            sums, *made = cell_quarter(info, counts, s, cell_turned, left, not got)
            sums, left = lax.optimization_barrier((sums, made or left))
            got[s] = shift(sums, "x", X, s) if s else sums
        gene_copy = left[0]
        part = kernel_call(four_sum_kernel, info, [got[s] for s in range(X)], struct((RANK, quarter + LANES)))
        got = [shift(part, "z_hi", n_zhi, s) for s in range(1, n_zhi)]
        new = kernel_call(cell_update_kernel, info, (cells[0], part, *got), struct((RANK, quarter)))
        cells = [new] + [shift(new, "x", X, s) for s in (1, 2, 3)]
    joined = kernel_call(join_genes_kernel, info, (mine, other), struct((GROUPS, 8, n_genes)))
    cells = kernel_call(join_cells_kernel, info, cells, struct((RANK, n_cells)))
    return cells, joined.reshape(RANK, n_genes)


def solution(mesh):
    n_z, n_zhi = mesh.shape["cell"] // (Y * CORES), mesh.shape["gene"] // X
    cut = Mesh(mesh.devices.reshape(n_z, Y, CORES, n_zhi, X), ("z", "y", "core", "z_hi", "x"))
    cell, gene = ("z", "y", "core"), ("z_hi", "x")
    return jax.shard_map(
        functools.partial(per_device, n_z, n_zhi),
        mesh=cut,
        in_specs=(P(cell, gene), P(None, cell), P(None, gene)),
        out_specs=(P(None, cell), P(None, gene)),
        check_vma=False,
    )
```

```python
import functools

import jax
import jax.numpy as jnp
from jax import lax
from jax.experimental import pallas as pl
from jax.experimental.pallas import tpu as pltpu
from jax.sharding import Mesh
from jax.sharding import PartitionSpec as P

ITERS = 3
RANK = 32
GROUPS = 4
LANES = 128
WIDE = 1024
CORES, Y, X = 2, 4, 4
SMALL_VMEM, PASS_VMEM = 4 << 20, 28 << 20
F32, BF16 = jnp.float32, jnp.bfloat16

AT_CORE, AT_Y, AT_Z, AT_X = range(4)


def struct(shape, dtype=F32):
    return jax.ShapeDtypeStruct(shape, dtype)


def kernel_call(kernel, info, operands, out_shape, scratch=(), vmem=SMALL_VMEM, cost=None):
    return pl.pallas_call(
        kernel,
        grid_spec=pltpu.PrefetchScalarGridSpec(
            num_scalar_prefetch=1,
            grid=(),
            in_specs=[pl.BlockSpec(memory_space=pltpu.VMEM)] * len(operands),
            out_specs=jax.tree.map(lambda _: pl.BlockSpec(memory_space=pltpu.VMEM), out_shape),
            scratch_shapes=list(scratch),
        ),
        out_shape=out_shape,
        compiler_params=pltpu.CompilerParams(vmem_limit_bytes=vmem),
        cost_estimate=cost,
    )(info, *operands)


def pass_cost(cells, genes):
    return pl.CostEstimate(flops=cells, bytes_accessed=genes, transcendentals=0)


def ratio_of(counts, approx):
    return (counts.astype(F32) * pl.reciprocal(approx, approx=True)).astype(BF16)


def span(index, size):
    return pl.ds(pl.multiple_of(index * size, size), size)


def fill_genes(refs, side, groups):
    (ref,) = refs
    half = groups.shape[2]
    if ref.shape[0] == GROUPS:
        groups[...] = ref[:, :, span(side, half)]
        return
    width = ref.shape[2]
    n_z = half // width
    for y in range(Y):
        for z in range(n_z):
            groups[y, :, z * width : (z + 1) * width] = ref[y * n_z + z]


def gene_block(counts_ref, rows, cols, turned, copy, genes):
    approx = jnp.dot(turned, genes, preferred_element_type=F32)
    ratio = ratio_of(counts_ref[rows, cols], approx)
    return jnp.dot(copy, ratio, preferred_element_type=F32)


def gene_quarter(s, info, counts_ref, piece, gene_copy, out_ref, begun_ref=None):
    n_genes = counts_ref.shape[1]
    rows = span(lax.rem(info[AT_X] + (X - s), X), piece.shape[1])
    copy, turned = piece.astype(BF16), piece.T.astype(BF16)
    for start in range(0, n_genes, WIDE):
        cols = slice(start, start + WIDE)
        numer = gene_block(counts_ref, rows, cols, turned, copy, gene_copy[:, cols])
        out_ref[:, cols] = numer if begun_ref is None else begun_ref[:, cols] + numer


def gene_start_kernel(info, counts_ref, cells_ref, genes_ref, out_ref, gene_copy, *piece_refs):
    for s, ref in enumerate(piece_refs):
        ref[...] = cells_ref[:, span(lax.rem(info[AT_X] + (X - s), X), ref.shape[1])]
    gene_copy[...] = genes_ref[...].reshape(RANK, counts_ref.shape[1]).astype(BF16)
    gene_quarter(0, info, counts_ref, piece_refs[0][...], gene_copy, out_ref)


def gene_own_kernel(info, counts_ref, piece_ref, gene_copy, out_ref):
    gene_quarter(0, info, counts_ref, piece_ref[...], gene_copy, out_ref)


def gene_next_kernel(info, counts_ref, piece_ref, gene_copy, begun_ref, out_ref):
    gene_quarter(X - 1, info, counts_ref, piece_ref[...], gene_copy, out_ref, begun_ref)


def gene_half(side, info, counts_ref, begun_ref, gene_copy, cell_copy, cell_turned, sums, out_ref):
    half = out_ref.shape[2] - LANES
    quarter = counts_ref.shape[0] // X
    cols = span(side, half)
    genes = gene_copy[:, cols]
    numer = begun_ref[:, cols]
    for s in range(1, X - 1):
        rows = span(lax.rem(info[AT_X] + (X - s), X), quarter)
        part = slice(s * quarter, (s + 1) * quarter)
        numer = numer + gene_block(counts_ref, rows, cols, cell_turned[part, :], cell_copy[:, part], genes)
    out_ref[:, :, :half] = numer.reshape(GROUPS, 8, half)
    out_ref[:, :, half:] = sums[...].reshape(GROUPS, 8, LANES)


def gene_first_kernel(info, counts_ref, begun_ref, gene_copy, f0, f1, f2, f3, out_ref, cell_copy, cell_turned, sums):
    total = jnp.zeros((RANK, 1), F32)
    for s, ref in enumerate((f0, f1, f2, f3)):
        piece = ref[...]
        part = slice(s * piece.shape[1], (s + 1) * piece.shape[1])
        cell_copy[:, part] = piece.astype(BF16)
        cell_turned[part, :] = piece.T.astype(BF16)
        total = total + jnp.sum(piece, axis=1, keepdims=True)
    sums[...] = jnp.broadcast_to(total, (RANK, LANES))
    gene_half(1 - info[AT_CORE], info, counts_ref, begun_ref, gene_copy, cell_copy, cell_turned, sums, out_ref)


def gene_second_kernel(info, counts_ref, begun_ref, gene_copy, cell_copy, cell_turned, sums, out_ref):
    gene_half(info[AT_CORE], info, counts_ref, begun_ref, gene_copy, cell_copy, cell_turned, sums, out_ref)


def pass_call(kernel, info, operands, out_shape, cells, genes, scratch=()):
    return kernel_call(kernel, info, operands, out_shape, scratch, PASS_VMEM, pass_cost(cells, genes))


def gene_pass(info, counts, begun, gene_copy, cells):
    n_cells, n_genes = counts.shape
    half = n_genes // CORES
    out = struct((GROUPS, 8, half + LANES))
    made = [struct((RANK, n_cells), BF16), struct((n_cells, RANK), BF16), struct((RANK, LANES))]
    sent, *made = pass_call(gene_first_kernel, info, (counts, begun, gene_copy, *cells), [out] + made, n_cells, half)
    own = lambda: pass_call(gene_second_kernel, info, (counts, begun, gene_copy, *made), out, n_cells, half)
    return sent, made[1], own


def tiles_of(quarter):
    return (GROUPS * (quarter // LANES) + 1, 8, LANES)


def put_tiles(out_ref, numer, sums):
    across = numer.shape[1] // LANES
    for g in range(GROUPS):
        for c in range(across):
            out_ref[g * across + c] = numer[8 * g : 8 * g + 8, c * LANES : (c + 1) * LANES]
    out_ref[GROUPS * across] = sums


def cell_rows(to, info, cell_turned, quarter):
    at = (X - to) % X * quarter
    return span(lax.rem(info[AT_X] + to, X), quarter), cell_turned[at : at + quarter, :]


def cell_block(counts_ref, rows, cols, cells, genes):
    approx = jnp.dot(cells, genes, preferred_element_type=F32)
    ratio = ratio_of(counts_ref[rows, cols], approx)
    return lax.dot_general(genes, ratio, (((1,), (1,)), ((), ())), preferred_element_type=F32)


def cell_begin_kernel(to, info, counts_ref, cell_turned, mine_ref, out_ref, groups):
    quarter, half = out_ref.shape[1], groups.shape[2]
    fill_genes([mine_ref], 0, groups)
    genes = groups[...].reshape(RANK, half).astype(BF16)
    rows, cells = cell_rows(to, info, cell_turned, quarter)
    out_ref[...] = cell_block(counts_ref, rows, span(info[AT_CORE], half), cells, genes)


def cell_first_kernel(
    to, info, counts_ref, cell_turned, begun_ref, mine_ref, other_ref, out_ref, gene_copy, sums, ordered
):
    half = ordered.shape[2] // CORES
    quarter = begun_ref.shape[1]
    for side, ref in ((info[AT_CORE], mine_ref), (1 - info[AT_CORE], other_ref)):
        fill_genes([ref], side, ordered.at[:, :, span(side, half)])
    factor = ordered[...].reshape(RANK, CORES * half)
    gene_copy[...] = factor.astype(BF16)
    total = jnp.broadcast_to(jnp.sum(factor, axis=1, keepdims=True), (RANK, LANES))
    sums[...] = jnp.concatenate([total] * (LANES // RANK), axis=0).T[:8]
    rows, cells = cell_rows(to, info, cell_turned, quarter)
    cols = span(1 - info[AT_CORE], half)
    numer = begun_ref[...] + cell_block(counts_ref, rows, cols, cells, gene_copy[:, cols])
    put_tiles(out_ref, numer, sums[...])


def cell_later_kernel(to, info, counts_ref, cell_turned, gene_copy, sums, out_ref):
    quarter = counts_ref.shape[0] // X
    rows, cells = cell_rows(to, info, cell_turned, quarter)
    numer = jnp.zeros((RANK, quarter), F32)
    for start in range(0, counts_ref.shape[1], WIDE):
        cols = slice(start, start + WIDE)
        numer = numer + cell_block(counts_ref, rows, cols, cells, gene_copy[:, cols])
    put_tiles(out_ref, numer, sums[...])


def cell_begin(info, counts, to, cell_turned, mine):
    n_cells, n_genes = counts.shape
    return pass_call(
        functools.partial(cell_begin_kernel, to),
        info,
        (counts, cell_turned, mine),
        struct((RANK, n_cells // X)),
        n_cells // X,
        n_genes // CORES,
        [pltpu.VMEM((GROUPS, 8, n_genes // CORES), F32)],
    )


def cell_quarter(info, counts, to, cell_turned, left, first):
    n_cells, n_genes = counts.shape
    quarter = n_cells // X
    sums = struct(tiles_of(quarter))
    made = [struct((RANK, n_genes), BF16), struct((8, LANES))]
    return pass_call(
        functools.partial(cell_first_kernel if first else cell_later_kernel, to),
        info,
        (counts, cell_turned, *left),
        [sums] + made if first else [sums],
        quarter,
        n_genes,
        [pltpu.VMEM((GROUPS, 8, n_genes), F32)] if first else [],
    )


def pair_sum_kernel(info, a_ref, b_ref, out_ref):
    width = out_ref.shape[2] - LANES
    half = a_ref.shape[2] - LANES
    n_z = half // width
    for y in range(Y):
        total = a_ref[y] + b_ref[y]
        for z in range(n_z):
            out_ref[y * n_z + z, :, :width] = total[:, z * width : (z + 1) * width]
            out_ref[y * n_z + z, :, width:] = total[:, half:]


def four_sum_kernel(info, a_ref, b_ref, c_ref, d_ref, out_ref):
    out_ref[...] = (a_ref[...] + b_ref[...]) + (c_ref[...] + d_ref[...])


def updated(piece, total):
    width = piece.shape[1]
    return piece * total[:, :width] / total[:, width : width + 1]


def gene_update_kernel(info, parts_ref, old_ref, new_ref, spread_ref):
    total = parts_ref[0]
    for i in range(1, parts_ref.shape[0]):
        total = total + parts_ref[i]
    width = new_ref.shape[1]
    if old_ref.ndim == 2:
        old = old_ref[...]
    else:
        n_z = parts_ref.shape[0] // Y
        old = old_ref[info[AT_Y], :, span(info[AT_CORE] * n_z + info[AT_Z], width)]
    new = updated(old, total)
    new_ref[...] = new
    for i in range(spread_ref.shape[0]):
        spread_ref[i] = new


def cell_update_kernel(info, old_ref, *refs):
    out_ref = refs[-1]
    total = refs[0][...]
    for ref in refs[1:-1]:
        total = total + ref[...]
    sums = jnp.concatenate([total[-1]] * (LANES // 8), axis=0).T
    across = out_ref.shape[1] // LANES
    for g in range(GROUPS):
        rows = slice(8 * g, 8 * g + 8)
        for c in range(across):
            cols = slice(c * LANES, (c + 1) * LANES)
            out_ref[rows, cols] = old_ref[rows, cols] * total[g * across + c] / sums[rows]


def join_genes_kernel(info, mine_ref, other_ref, out_ref):
    half = out_ref.shape[2] // CORES
    for side, ref in ((info[AT_CORE], mine_ref), (1 - info[AT_CORE], other_ref)):
        fill_genes([ref], side, out_ref.at[:, :, span(side, half)])


def join_cells_kernel(info, *refs):
    for s, ref in enumerate(refs[:-1]):
        refs[-1][:, span(lax.rem(info[AT_X] + (X - s), X), ref.shape[1])] = ref[...]


def per_device(n_z, n_zhi, counts, cell_factor, gene_factor):
    n_cells, n_genes = counts.shape
    half, quarter, width = n_genes // CORES, n_cells // X, n_genes // (CORES * n_z)
    info = jnp.stack([lax.axis_index(a) for a in ("core", "y", "z", "x")]).astype(jnp.int32)
    swap = lambda a: lax.all_to_all(a, ("y", "z"), 0, 0, tiled=True)
    shift = lambda a, axis, n, s: lax.ppermute(a, axis, [(i, (i + s) % n) for i in range(n)])

    piece = gene_factor.reshape(GROUPS, 8, n_genes)
    begun, gene_copy, *cells = pass_call(
        gene_start_kernel,
        info,
        (counts, cell_factor, piece),
        [struct((RANK, n_genes)), struct((RANK, n_genes), BF16)] + [struct((RANK, quarter))] * X,
        quarter,
        n_genes,
    )
    for step in range(ITERS):
        if step:
            begun = pass_call(
                gene_own_kernel, info, (counts, cells[0], gene_copy), struct((RANK, n_genes)), quarter, n_genes
            )
        begun = pass_call(
            gene_next_kernel,
            info,
            (counts, cells[X - 1], gene_copy, begun),
            struct((RANK, n_genes)),
            quarter,
            n_genes,
        )
        sent, cell_turned, own = gene_pass(info, counts, begun, gene_copy, cells)
        got = shift(sent, "core", CORES, 1)
        kept = own()
        parts = kernel_call(pair_sum_kernel, info, (kept, got), struct((Y * n_z, 8, width + LANES)))
        piece, spread = kernel_call(
            gene_update_kernel, info, (swap(parts), piece), [struct((8, width)), struct((Y * n_z, 8, width))]
        )
        mine = swap(spread)
        other = shift(mine, "core", CORES, 1)

        left = (cell_begin(info, counts, 2, cell_turned, mine), mine, other)
        got = {}
        for s in (2, 1, 3, 0):
            sums, *made = cell_quarter(info, counts, s, cell_turned, left, not got)
            sums, left = lax.optimization_barrier((sums, made or left))
            got[s] = shift(sums, "x", X, s) if s else sums
        gene_copy = left[0]
        part = kernel_call(four_sum_kernel, info, [got[s] for s in range(X)], struct(tiles_of(quarter)))
        got = [shift(part, "z_hi", n_zhi, s) for s in range(1, n_zhi)]
        new = kernel_call(cell_update_kernel, info, (cells[0], part, *got), struct((RANK, quarter)))
        cells = [new] + [shift(new, "x", X, s) for s in (1, 2, 3)]
    joined = kernel_call(join_genes_kernel, info, (mine, other), struct((GROUPS, 8, n_genes)))
    cells = kernel_call(join_cells_kernel, info, cells, struct((RANK, n_cells)))
    return cells, joined.reshape(RANK, n_genes)


def solution(mesh):
    n_z, n_zhi = mesh.shape["cell"] // (Y * CORES), mesh.shape["gene"] // X
    cut = Mesh(mesh.devices.reshape(n_z, Y, CORES, n_zhi, X), ("z", "y", "core", "z_hi", "x"))
    cell, gene = ("z", "y", "core"), ("z_hi", "x")
    return jax.shard_map(
        functools.partial(per_device, n_z, n_zhi),
        mesh=cut,
        in_specs=(P(cell, gene), P(None, cell), P(None, gene)),
        out_specs=(P(None, cell), P(None, gene)),
        check_vma=False,
    )
```

```python
import functools

import jax
import jax.numpy as jnp
from jax import lax
from jax.experimental import pallas as pl
from jax.experimental.pallas import tpu as pltpu
from jax.sharding import Mesh
from jax.sharding import PartitionSpec as P

ITERS = 3
RANK = 32
GROUPS = 4
LANES = 128
WIDE = 1024
CORES, Y, X = 2, 4, 4
SMALL_VMEM, PASS_VMEM = 4 << 20, 28 << 20
F32, BF16 = jnp.float32, jnp.bfloat16

AT_CORE, AT_Y, AT_Z, AT_X = range(4)


def struct(shape, dtype=F32):
    return jax.ShapeDtypeStruct(shape, dtype)


def kernel_call(kernel, info, operands, out_shape, scratch=(), vmem=SMALL_VMEM, cost=None):
    return pl.pallas_call(
        kernel,
        grid_spec=pltpu.PrefetchScalarGridSpec(
            num_scalar_prefetch=1,
            grid=(),
            in_specs=[pl.BlockSpec(memory_space=pltpu.VMEM)] * len(operands),
            out_specs=jax.tree.map(lambda _: pl.BlockSpec(memory_space=pltpu.VMEM), out_shape),
            scratch_shapes=list(scratch),
        ),
        out_shape=out_shape,
        compiler_params=pltpu.CompilerParams(vmem_limit_bytes=vmem),
        cost_estimate=cost,
    )(info, *operands)


def pass_cost(cells, genes):
    return pl.CostEstimate(flops=cells, bytes_accessed=genes, transcendentals=0)


def ratio_of(counts, approx):
    return (counts.astype(F32) * pl.reciprocal(approx, approx=True)).astype(BF16)


def span(index, size):
    return pl.ds(pl.multiple_of(index * size, size), size)


def fill_genes(refs, side, groups):
    (ref,) = refs
    half = groups.shape[2]
    if ref.shape[0] == GROUPS:
        groups[...] = ref[:, :, span(side, half)]
        return
    width = ref.shape[2]
    n_z = half // width
    for y in range(Y):
        for z in range(n_z):
            groups[y, :, z * width : (z + 1) * width] = ref[y * n_z + z]


def gene_block(counts_ref, rows, cols, turned, copy, genes):
    approx = jnp.dot(turned, genes, preferred_element_type=F32)
    ratio = ratio_of(counts_ref[rows, cols], approx)
    return jnp.dot(copy, ratio, preferred_element_type=F32)


def gene_quarter(s, info, counts_ref, piece, gene_copy, out_ref, begun_ref=None):
    n_genes = counts_ref.shape[1]
    rows = span(lax.rem(info[AT_X] + (X - s), X), piece.shape[1])
    copy, turned = piece.astype(BF16), piece.T.astype(BF16)
    for start in range(0, n_genes, WIDE):
        cols = slice(start, start + WIDE)
        numer = gene_block(counts_ref, rows, cols, turned, copy, gene_copy[:, cols])
        out_ref[:, cols] = numer if begun_ref is None else begun_ref[:, cols] + numer


def gene_start_kernel(info, counts_ref, cells_ref, genes_ref, out_ref, gene_copy, *piece_refs):
    for s, ref in enumerate(piece_refs):
        ref[...] = cells_ref[:, span(lax.rem(info[AT_X] + (X - s), X), ref.shape[1])]
    gene_copy[...] = genes_ref[...].reshape(RANK, counts_ref.shape[1]).astype(BF16)
    gene_quarter(0, info, counts_ref, piece_refs[0][...], gene_copy, out_ref)


def gene_own_kernel(info, counts_ref, piece_ref, gene_copy, out_ref):
    gene_quarter(0, info, counts_ref, piece_ref[...], gene_copy, out_ref)


def gene_next_kernel(info, counts_ref, piece_ref, gene_copy, begun_ref, out_ref):
    gene_quarter(X - 1, info, counts_ref, piece_ref[...], gene_copy, out_ref, begun_ref)


def gene_half(side, info, counts_ref, begun_ref, gene_copy, cell_copy, cell_turned, sums, out_ref):
    half = out_ref.shape[2] - LANES
    quarter = counts_ref.shape[0] // X
    cols = span(side, half)
    genes = gene_copy[:, cols]
    numer = begun_ref[:, cols]
    for s in range(1, X - 1):
        rows = span(lax.rem(info[AT_X] + (X - s), X), quarter)
        part = slice(s * quarter, (s + 1) * quarter)
        numer = numer + gene_block(counts_ref, rows, cols, cell_turned[part, :], cell_copy[:, part], genes)
    out_ref[:, :, :half] = numer.reshape(GROUPS, 8, half)
    out_ref[:, :, half:] = sums[...].reshape(GROUPS, 8, LANES)


def gene_first_kernel(info, counts_ref, begun_ref, gene_copy, f0, f1, f2, f3, out_ref, cell_copy, cell_turned, sums):
    total = jnp.zeros((RANK, 1), F32)
    for s, ref in enumerate((f0, f1, f2, f3)):
        piece = ref[...]
        part = slice(s * piece.shape[1], (s + 1) * piece.shape[1])
        cell_copy[:, part] = piece.astype(BF16)
        cell_turned[part, :] = piece.T.astype(BF16)
        total = total + jnp.sum(piece, axis=1, keepdims=True)
    sums[...] = jnp.broadcast_to(total, (RANK, LANES))
    gene_half(1 - info[AT_CORE], info, counts_ref, begun_ref, gene_copy, cell_copy, cell_turned, sums, out_ref)


def gene_second_kernel(info, counts_ref, begun_ref, gene_copy, cell_copy, cell_turned, sums, out_ref):
    gene_half(info[AT_CORE], info, counts_ref, begun_ref, gene_copy, cell_copy, cell_turned, sums, out_ref)


def pass_call(kernel, info, operands, out_shape, cells, genes, scratch=()):
    return kernel_call(kernel, info, operands, out_shape, scratch, PASS_VMEM, pass_cost(cells, genes))


def gene_pass(info, counts, begun, gene_copy, cells):
    n_cells, n_genes = counts.shape
    half = n_genes // CORES
    out = struct((GROUPS, 8, half + LANES))
    made = [struct((RANK, n_cells), BF16), struct((n_cells, RANK), BF16), struct((RANK, LANES))]
    sent, *made = pass_call(gene_first_kernel, info, (counts, begun, gene_copy, *cells), [out] + made, n_cells, half)
    own = lambda: pass_call(gene_second_kernel, info, (counts, begun, gene_copy, *made), out, n_cells, half)
    return sent, made[1], own


def tiles_of(quarter):
    return (GROUPS * (quarter // LANES) + 1, 8, LANES)


def put_tiles(out_ref, numer, sums):
    across = numer.shape[1] // LANES
    for g in range(GROUPS):
        for c in range(across):
            out_ref[g * across + c] = numer[8 * g : 8 * g + 8, c * LANES : (c + 1) * LANES]
    out_ref[GROUPS * across] = sums


def cell_rows(to, info, cell_turned, quarter):
    at = (X - to) % X * quarter
    return span(lax.rem(info[AT_X] + to, X), quarter), cell_turned[at : at + quarter, :]


def cell_block(counts_ref, rows, cols, cells, genes):
    approx = jnp.dot(cells, genes, preferred_element_type=F32)
    ratio = ratio_of(counts_ref[rows, cols], approx)
    return lax.dot_general(genes, ratio, (((1,), (1,)), ((), ())), preferred_element_type=F32)


def cell_begin_kernel(to, info, counts_ref, cell_turned, mine_ref, out_ref, groups):
    quarter, half = out_ref.shape[1], groups.shape[2]
    fill_genes([mine_ref], 0, groups)
    genes = groups[...].reshape(RANK, half).astype(BF16)
    rows, cells = cell_rows(to, info, cell_turned, quarter)
    out_ref[...] = cell_block(counts_ref, rows, span(info[AT_CORE], half), cells, genes)


def cell_first_kernel(
    to, info, counts_ref, cell_turned, begun_ref, mine_ref, other_ref, out_ref, gene_copy, sums, ordered
):
    half = ordered.shape[2] // CORES
    quarter = begun_ref.shape[1]
    for side, ref in ((info[AT_CORE], mine_ref), (1 - info[AT_CORE], other_ref)):
        fill_genes([ref], side, ordered.at[:, :, span(side, half)])
    factor = ordered[...].reshape(RANK, CORES * half)
    gene_copy[...] = factor.astype(BF16)
    total = jnp.broadcast_to(jnp.sum(factor, axis=1, keepdims=True), (RANK, LANES))
    sums[...] = jnp.concatenate([total] * (LANES // RANK), axis=0).T[:8]
    rows, cells = cell_rows(to, info, cell_turned, quarter)
    cols = span(1 - info[AT_CORE], half)
    numer = begun_ref[...] + cell_block(counts_ref, rows, cols, cells, gene_copy[:, cols])
    put_tiles(out_ref, numer, sums[...])


def cell_later_kernel(to, info, counts_ref, cell_turned, gene_copy, sums, *refs):
    arrived, out_ref = refs[:-1], refs[-1]
    quarter = counts_ref.shape[0] // X
    rows, cells = cell_rows(to, info, cell_turned, quarter)
    numer = jnp.zeros((RANK, quarter), F32)
    for start in range(0, counts_ref.shape[1], WIDE):
        cols = slice(start, start + WIDE)
        numer = numer + cell_block(counts_ref, rows, cols, cells, gene_copy[:, cols])
    put_tiles(out_ref, numer, sums[...])
    for ref in arrived:
        out_ref[...] = out_ref[...] + ref[...]


def cell_begin(info, counts, to, cell_turned, mine):
    n_cells, n_genes = counts.shape
    return pass_call(
        functools.partial(cell_begin_kernel, to),
        info,
        (counts, cell_turned, mine),
        struct((RANK, n_cells // X)),
        n_cells // X,
        n_genes // CORES,
        [pltpu.VMEM((GROUPS, 8, n_genes // CORES), F32)],
    )


def cell_quarter(info, counts, to, cell_turned, left, first):
    n_cells, n_genes = counts.shape
    quarter = n_cells // X
    sums = struct(tiles_of(quarter))
    made = [struct((RANK, n_genes), BF16), struct((8, LANES))]
    return pass_call(
        functools.partial(cell_first_kernel if first else cell_later_kernel, to),
        info,
        (counts, cell_turned, *left),
        [sums] + made if first else [sums],
        quarter,
        n_genes,
        [pltpu.VMEM((GROUPS, 8, n_genes), F32)] if first else [],
    )


def pair_sum_kernel(info, a_ref, b_ref, out_ref):
    width = out_ref.shape[2] - LANES
    half = a_ref.shape[2] - LANES
    n_z = half // width
    for y in range(Y):
        total = a_ref[y] + b_ref[y]
        for z in range(n_z):
            out_ref[y * n_z + z, :, :width] = total[:, z * width : (z + 1) * width]
            out_ref[y * n_z + z, :, width:] = total[:, half:]


def three_sum_kernel(info, a_ref, b_ref, c_ref, out_ref):
    out_ref[...] = a_ref[...] + (b_ref[...] + c_ref[...])


def updated(piece, total):
    width = piece.shape[1]
    return piece * total[:, :width] / total[:, width : width + 1]


def gene_update_kernel(info, parts_ref, old_ref, new_ref, spread_ref):
    total = parts_ref[0]
    for i in range(1, parts_ref.shape[0]):
        total = total + parts_ref[i]
    width = new_ref.shape[1]
    if old_ref.ndim == 2:
        old = old_ref[...]
    else:
        n_z = parts_ref.shape[0] // Y
        old = old_ref[info[AT_Y], :, span(info[AT_CORE] * n_z + info[AT_Z], width)]
    new = updated(old, total)
    new_ref[...] = new
    for i in range(spread_ref.shape[0]):
        spread_ref[i] = new


def cell_update_kernel(info, old_ref, *refs):
    out_ref = refs[-1]
    total = refs[0][...]
    for ref in refs[1:-1]:
        total = total + ref[...]
    sums = jnp.concatenate([total[-1]] * (LANES // 8), axis=0).T
    across = out_ref.shape[1] // LANES
    for g in range(GROUPS):
        rows = slice(8 * g, 8 * g + 8)
        for c in range(across):
            cols = slice(c * LANES, (c + 1) * LANES)
            out_ref[rows, cols] = old_ref[rows, cols] * total[g * across + c] / sums[rows]


def join_genes_kernel(info, mine_ref, other_ref, out_ref):
    half = out_ref.shape[2] // CORES
    for side, ref in ((info[AT_CORE], mine_ref), (1 - info[AT_CORE], other_ref)):
        fill_genes([ref], side, out_ref.at[:, :, span(side, half)])


def join_cells_kernel(info, *refs):
    for s, ref in enumerate(refs[:-1]):
        refs[-1][:, span(lax.rem(info[AT_X] + (X - s), X), ref.shape[1])] = ref[...]


def per_device(n_z, n_zhi, counts, cell_factor, gene_factor):
    n_cells, n_genes = counts.shape
    half, quarter, width = n_genes // CORES, n_cells // X, n_genes // (CORES * n_z)
    info = jnp.stack([lax.axis_index(a) for a in ("core", "y", "z", "x")]).astype(jnp.int32)
    swap = lambda a: lax.all_to_all(a, ("y", "z"), 0, 0, tiled=True)
    shift = lambda a, axis, n, s: lax.ppermute(a, axis, [(i, (i + s) % n) for i in range(n)])

    piece = gene_factor.reshape(GROUPS, 8, n_genes)
    begun, gene_copy, *cells = pass_call(
        gene_start_kernel,
        info,
        (counts, cell_factor, piece),
        [struct((RANK, n_genes)), struct((RANK, n_genes), BF16)] + [struct((RANK, quarter))] * X,
        quarter,
        n_genes,
    )
    for step in range(ITERS):
        if step:
            begun = pass_call(
                gene_own_kernel, info, (counts, cells[0], gene_copy), struct((RANK, n_genes)), quarter, n_genes
            )
        begun = pass_call(
            gene_next_kernel,
            info,
            (counts, cells[X - 1], gene_copy, begun),
            struct((RANK, n_genes)),
            quarter,
            n_genes,
        )
        sent, cell_turned, own = gene_pass(info, counts, begun, gene_copy, cells)
        got = shift(sent, "core", CORES, 1)
        kept = own()
        parts = kernel_call(pair_sum_kernel, info, (kept, got), struct((Y * n_z, 8, width + LANES)))
        piece, spread = kernel_call(
            gene_update_kernel, info, (swap(parts), piece), [struct((8, width)), struct((Y * n_z, 8, width))]
        )
        mine = swap(spread)
        other = shift(mine, "core", CORES, 1)

        left = (cell_begin(info, counts, 2, cell_turned, mine), mine, other)
        got = {}
        for s in (2, 1, 3, 0):
            sums, *made = cell_quarter(info, counts, s, cell_turned, left if s else (*left, got[2]), not got)
            sums, left = lax.optimization_barrier((sums, made or left))
            got[s] = shift(sums, "x", X, s) if s else sums
        gene_copy = left[0]
        part = kernel_call(three_sum_kernel, info, [got[s] for s in (0, 1, 3)], struct(tiles_of(quarter)))
        got = [shift(part, "z_hi", n_zhi, s) for s in range(1, n_zhi)]
        new = kernel_call(cell_update_kernel, info, (cells[0], part, *got), struct((RANK, quarter)))
        cells = [new] + [shift(new, "x", X, s) for s in (1, 2, 3)]
    joined = kernel_call(join_genes_kernel, info, (mine, other), struct((GROUPS, 8, n_genes)))
    cells = kernel_call(join_cells_kernel, info, cells, struct((RANK, n_cells)))
    return cells, joined.reshape(RANK, n_genes)


def solution(mesh):
    n_z, n_zhi = mesh.shape["cell"] // (Y * CORES), mesh.shape["gene"] // X
    cut = Mesh(mesh.devices.reshape(n_z, Y, CORES, n_zhi, X), ("z", "y", "core", "z_hi", "x"))
    cell, gene = ("z", "y", "core"), ("z_hi", "x")
    return jax.shard_map(
        functools.partial(per_device, n_z, n_zhi),
        mesh=cut,
        in_specs=(P(cell, gene), P(None, cell), P(None, gene)),
        out_specs=(P(None, cell), P(None, gene)),
        check_vma=False,
    )
```
